32 devices in a mesh: pipe: 4 (over y, x), dp: 8 (over z, core).
Axes of the slice: x: 2, y: 2, z: 4, core: 2. Of those that a mesh axis runs over, the one named last changes fastest.
Arguments:
- inputs: bfloat16 [4, 64, 8192], P('pipe', 'dp'), may hold values from -6 to 6
- cotangent: bfloat16 [4, 64, 8192], P('pipe', 'dp'), may hold values from -6 to 6
- norm_gain: float32 [4, 8192], P('pipe'), may hold values from 0.1 to 1.9
- w_value: bfloat16 [4, 64, 8192], P('pipe'), may hold values from -0.0625 to 0.0625
- w_out: bfloat16 [4, 64, 8192], P('pipe'), may hold values from -0.75 to 0.75
- value_down: bfloat16 [4, 8, 16, 8192], P('pipe', 'dp'), may hold values from -0.0625 to 0.0625
- value_up_factor: bfloat16 [4, 8, 16, 64], P('pipe', 'dp'), may hold values from -1.5 to 1.5
- out_down: bfloat16 [4, 8, 16, 64], P('pipe', 'dp'), may hold values from -0.75 to 0.75
- output_up_factor: bfloat16 [4, 8, 16, 8192], P('pipe', 'dp'), may hold values from -1.5 to 1.5
- block_tenant: int32 [8], replicated, may hold values from 0 to 7
- valid_tokens: int32 [8], replicated, may hold values from 1 to 32, 192 in all
- tenant_slot: int32 [8], replicated, may hold values from 0 to 7, each once
Outputs:
- grad_value_down: bfloat16 [4, 8, 16, 8192], P('pipe', 'dp')
- grad_value_up: bfloat16 [4, 8, 16, 64], P('pipe', 'dp')
- grad_out_down: bfloat16 [4, 8, 16, 64], P('pipe', 'dp')
- grad_out_up: bfloat16 [4, 8, 16, 8192], P('pipe', 'dp')
The draws below stay inside these ranges and needn't reach their ends.
Inputs may be any that keep to these rules, and one draw needn't show every extreme that they name: `block_tenant`: tenant whose adapters serve all 32 tokens of a dp index. The first valid_tokens[i] block positions of dp index i are valid, the rest padding. A permutation: the adapters and gradients of tenant t sit at slot tenant_slot[t], stored on dp index tenant_slot[t].
All inputs are finite; a program needn't handle non-finite values.
Results may differ from the reference program's by a relative error of at most 0.034.
Values may be sent and summed in bfloat16 or wider, within the bound.
A program may use at most 64 MiB of HBM per device.

```python
import math
import jax
import jax.numpy as jnp
import numpy as np
from jax import lax

D = 8192
HD = 64
RANK = 16
TOK = 8
LAYERS = 4
MICRO = 4
TENANTS = 8
TOKENS = 64
BLOCK = 32
N_DP = 8


def place_ends(drawn, rng, least, top_value):
    index_at = [jax.random.randint(jax.random.fold_in(rng, axis), (), 0, length) for axis, length in enumerate(drawn.shape)]
    main_axis = drawn.shape.index(max(drawn.shape))
    next_to = index_at[:main_axis] + [(index_at[main_axis] + 1) % drawn.shape[main_axis]] + index_at[main_axis + 1:]
    return drawn.at[tuple(index_at)].set(least).at[tuple(next_to)].set(top_value)


def block_scale(rng, shape, shards, least, high):
    gain, own = 1.0, jax.random.fold_in(rng, 6)
    for dim, parts in shards:
        heights = jnp.exp(jax.random.uniform(jax.random.fold_in(own, dim), (parts,), jnp.float32, least / len(shards), high / len(shards)))
        gain = gain * jnp.repeat(heights, shape[dim] // parts).reshape([-1 if axis == dim else 1 for axis in range(len(shape))])
    return gain


def cumulative_ranks(count, lean):
    weights = [(1 << 20) // math.isqrt(grade ** lean) + 1 for grade in range(1, count + 1)]
    width = 1 + sum(weights) // (1 << 30)
    return np.cumsum(np.array([max(1, weight // width) for weight in weights]))


def skewed_ids(key, extent, amount, skew):
    grid = cumulative_ranks(amount, skew)
    ticket = jax.random.randint(jax.random.fold_in(key, 1), extent, 0, int(grid[amount - 1]))
    standing = jnp.searchsorted(jnp.asarray(grid, jnp.int32), ticket, side="right")
    return jax.random.permutation(jax.random.fold_in(key, 2), amount)[standing].astype(jnp.int32)


def length_profile(count, total, bound, slope):
    portions = [(1 << 20) // math.isqrt(grade ** slope) + 1 for grade in range(2, count + 1)]
    rest, holding = total - bound - (count - 1), [1] * (count - 1)
    while rest > 0:
        movable = [i for i in range(count - 1) if holding[i] < bound]
        whole, left = sum([portions[i] for i in movable]), rest
        for i in movable:
            addition = min(bound - holding[i], max(1, left * portions[i] // whole), rest)
            holding[i] = holding[i] + addition
            rest = rest - addition
    return np.array([bound] + holding)


def uneven_parts(own_key, number_of, total, bound, slope):
    if number_of == 2:
        one = jax.random.randint(own_key, (), max(1, total - bound), min(bound, total - 1) + 1)
        return jnp.stack([one, total - one])
    lengths = jnp.asarray(length_profile(number_of, total, bound, slope), jnp.int32)
    couples = (number_of - 1) // 2
    donor, taker = lengths[1:1 + 2 * couples:2], lengths[2:2 + 2 * couples:2]
    slack = jnp.minimum(donor - 1, bound - taker)
    shifted = jax.random.randint(jax.random.fold_in(own_key, 1), (couples,), 0, 1 << 20) % (slack + 1)
    lengths = lengths.at[1:1 + 2 * couples:2].set(donor - shifted).at[2:2 + 2 * couples:2].set(taker + shifted)
    return lengths[jax.random.permutation(jax.random.fold_in(own_key, 2), number_of)]


def gaussian(key, extent, spread, limit, pieces=(), held_as=jnp.bfloat16):
    array = jax.random.normal(key, extent, jnp.float32) * spread
    if len(pieces) > 0:
        array = block_scale(key, extent, pieces, -0.22, 0.18) * array
    return jnp.clip(array, min=-limit, max=limit).astype(held_as)


def setup_inputs(seed: int = 0) -> dict:
    arg_keys = jax.random.split(jax.random.key(seed), 13)
    inputs = gaussian(arg_keys[0], (MICRO, TOKENS, D), 1.0, 6.0, ((0, 4), (1, 8)))
    cotangent = gaussian(arg_keys[1], (MICRO, TOKENS, D), 1.0, 6.0, ((0, 4), (1, 8)))
    norm_gain = jnp.clip(1.0 + 0.18 * jax.random.normal(arg_keys[2], (LAYERS, D), jnp.float32), 0.1, 1.9)
    w_value = gaussian(arg_keys[3], (LAYERS, HD, D), D ** -0.5, 0.0625, ((0, 4),))
    w_out = gaussian(arg_keys[4], (LAYERS, HD, D), HD ** -0.5, 0.75, ((0, 4),))
    value_down = gaussian(arg_keys[5], (LAYERS, TENANTS, RANK, D), D ** -0.5, 0.0625, ((0, 4), (1, 8)))
    value_up_factor = gaussian(arg_keys[6], (LAYERS, TENANTS, RANK, HD), RANK ** -0.5, 1.5, ((0, 4), (1, 8)))
    out_down = gaussian(arg_keys[7], (LAYERS, TENANTS, RANK, HD), HD ** -0.5, 0.75, ((0, 4), (1, 8)))
    output_up_factor = gaussian(arg_keys[8], (LAYERS, TENANTS, RANK, D), RANK ** -0.5, 1.5, ((0, 4), (1, 8)))
    block_tenant = place_ends(skewed_ids(arg_keys[9], (N_DP,), TENANTS, 2), jax.random.fold_in(arg_keys[9], 3), 0, TENANTS - 1).astype(jnp.int32)
    valid_tokens = uneven_parts(arg_keys[10], N_DP, N_DP * BLOCK * 3 // 4, BLOCK, 2).astype(jnp.int32)
    tenant_slot = jax.random.permutation(arg_keys[11], TENANTS).astype(jnp.int32)
    return {"inputs": inputs, "cotangent": cotangent, "norm_gain": norm_gain, "w_value": w_value, "w_out": w_out, "value_down": value_down, "value_up_factor": value_up_factor, "out_down": out_down, "output_up_factor": output_up_factor, "block_tenant": block_tenant, "valid_tokens": valid_tokens, "tenant_slot": tenant_slot}


adapter_scale = 2.0
norm_eps = 1e-05

def normalize(token_rows, gain_row):
    wide_rows = token_rows.astype(jnp.float32)
    inverse = lax.rsqrt(lax.optimization_barrier(jnp.mean(wide_rows * wide_rows, axis=-1, keepdims=True)) + norm_eps)
    return ((wide_rows * inverse * gain_row).astype(jnp.bfloat16), inverse)

def contract_trailing(left, right):
    return lax.dot_general(left, right, (((1,), (1,)), ((), ())), preferred_element_type=jnp.float32)

def contract_leading(left, right):
    return lax.dot_general(left, right, (((0,), (0,)), ((), ())), preferred_element_type=jnp.float32)

def section_parts(token_rows, gain_row, value_weight, tenant_adapters):
    value_down, value_up_factor, out_down, output_up_factor = tenant_adapters
    normalized_rows, inverse = normalize(token_rows, gain_row)
    lowrank_product = contract_trailing(normalized_rows, value_down).astype(jnp.bfloat16)
    value_blend = contract_trailing(normalized_rows, value_weight)
    value_blend = value_blend + adapter_scale * jnp.dot(lowrank_product, value_up_factor, preferred_element_type=jnp.float32)
    value_row_block = value_blend.astype(jnp.bfloat16)
    sidepath_rank = contract_trailing(value_row_block, out_down).astype(jnp.bfloat16)
    return (normalized_rows, inverse, lowrank_product, value_row_block, sidepath_rank)

def section_output(token_rows, layer_pieces, out_weight, tenant_adapters):
    blended_rows = token_rows.astype(jnp.float32) + jnp.dot(layer_pieces[3], out_weight, preferred_element_type=jnp.float32)
    blended_rows = blended_rows + adapter_scale * jnp.dot(layer_pieces[4], tenant_adapters[3], preferred_element_type=jnp.float32)
    return blended_rows.astype(jnp.bfloat16)

def section_backward(token_rows, input_gradient, layer_pieces, gain_row, value_weight, out_weight, tenant_adapters):
    value_down, value_up_factor, out_down, output_up_factor = tenant_adapters
    normalized_rows, inverse, lowrank_product, value_row_block, sidepath_rank = layer_pieces
    sidepath_gradient = (adapter_scale * contract_trailing(input_gradient, output_up_factor)).astype(jnp.bfloat16)
    value_gradient = contract_trailing(input_gradient, out_weight)
    value_gradient = (value_gradient + jnp.dot(sidepath_gradient, out_down, preferred_element_type=jnp.float32)).astype(jnp.bfloat16)
    lowrank_gradient = (adapter_scale * contract_trailing(value_gradient, value_up_factor)).astype(jnp.bfloat16)
    grad_normed = jnp.dot(value_gradient, value_weight, preferred_element_type=jnp.float32) + jnp.dot(lowrank_gradient, value_down, preferred_element_type=jnp.float32)
    scaled = grad_normed * gain_row
    wide_rows = token_rows.astype(jnp.float32)
    correction = lax.optimization_barrier(jnp.mean(scaled * wide_rows, axis=-1, keepdims=True))
    grad_rows = inverse * scaled - wide_rows * (inverse * inverse * inverse) * correction
    grad_out = (input_gradient.astype(jnp.float32) + grad_rows).astype(jnp.bfloat16)
    gradient_pieces = (contract_leading(lowrank_gradient, normalized_rows), adapter_scale * contract_leading(lowrank_product, value_gradient), contract_leading(sidepath_gradient, value_row_block), adapter_scale * contract_leading(sidepath_rank, input_gradient))
    return (grad_out, gradient_pieces)

def reference(inputs, cotangent, norm_gain, w_value, w_out, value_down, value_up_factor, out_down, output_up_factor, block_tenant, valid_tokens, tenant_slot):
    tenant_ids = jnp.arange(TENANTS, dtype=jnp.int32)
    tenant_hot = block_tenant[:, None] == tenant_ids[None, :]
    slot_of = lax.optimization_barrier(jnp.sum(jnp.where(tenant_hot, tenant_slot[None, :], 0), axis=1)).astype(jnp.int32)
    slot_hot = (slot_of[:, None] == tenant_ids[None, :]).astype(jnp.float32)
    same_tenant = block_tenant[:, None] == block_tenant[None, :]
    tenant_tokens = lax.optimization_barrier(jnp.sum(jnp.where(same_tenant, valid_tokens[None, :], 0), axis=1)).astype(jnp.float32)
    adapters_used = tuple((jnp.take(adapter_table, slot_of, axis=1) for adapter_table in (value_down, value_up_factor, out_down, output_up_factor)))
    parts_all = jax.vmap(section_parts, in_axes=(0, None, None, 0))
    output_all = jax.vmap(section_output, in_axes=(0, 0, None, 0))
    backward_all = jax.vmap(section_backward, in_axes=(0, 0, 0, None, None, None, 0))

    def micro_step(carry, micro_index):
        token_rows = lax.dynamic_index_in_dim(inputs, micro_index, 0, keepdims=False).reshape(N_DP, TOK, D)
        stored = []
        for layer_index in range(LAYERS):
            tenant_adapters = tuple((adapter_table[layer_index] for adapter_table in adapters_used))
            layer_pieces = parts_all(token_rows, norm_gain[layer_index], w_value[layer_index], tenant_adapters)
            stored.append((token_rows, layer_pieces))
            token_rows = output_all(token_rows, layer_pieces, w_out[layer_index], tenant_adapters)
        position = micro_index * TOK + jnp.arange(TOK, dtype=jnp.int32)
        weight = jnp.where(position[None, :] < valid_tokens[:, None], 1.0, 0.0).astype(jnp.float32) / tenant_tokens[:, None]
        seed_rows = lax.dynamic_index_in_dim(cotangent, micro_index, 0, keepdims=False).reshape(N_DP, TOK, D)
        grad_rows = (seed_rows.astype(jnp.float32) * weight[:, :, None]).astype(jnp.bfloat16)
        layer_terms = [None] * LAYERS
        for layer_index in reversed(range(LAYERS)):
            tenant_adapters = tuple((adapter_table[layer_index] for adapter_table in adapters_used))
            grad_rows, gradient_pieces = backward_all(stored[layer_index][0], grad_rows, stored[layer_index][1], norm_gain[layer_index], w_value[layer_index], w_out[layer_index], tenant_adapters)
            layer_terms[layer_index] = gradient_pieces
        stacked = tuple((jnp.stack([layer_terms[layer_index][term_index] for layer_index in range(LAYERS)]) for term_index in range(4)))
        return (tuple((running + addend for running, addend in zip(carry, stacked))), None)
    start = tuple((jnp.zeros((LAYERS, N_DP, RANK, column_count), jnp.float32) for column_count in (D, HD, HD, D)))
    totals, _ = lax.scan(micro_step, start, jnp.arange(MICRO, dtype=jnp.int32))

    def owner_sum(per_member):
        return jnp.einsum('ns,nrw->srw', slot_hot, per_member, precision=lax.Precision.HIGHEST).astype(jnp.bfloat16)
    return (lax.map(owner_sum, totals[0]), lax.map(owner_sum, totals[1]), lax.map(owner_sum, totals[2]), lax.map(owner_sum, totals[3]))
```

```python
import jax
import jax.numpy as jnp
from jax import lax
from jax.sharding import PartitionSpec as P

adapter_scale = 2.0
norm_eps = 1e-05
stash_limit = 8 * 2**20


def from_behind(value, axis, by):
    peers = lax.axis_size(axis)
    return lax.ppermute(value, axis, [(i, (i + by) % peers) for i in range(peers)])


def normalize(token_rows, gain_row):
    wide_rows = token_rows.astype(jnp.float32)
    inverse = lax.rsqrt(jnp.mean(wide_rows * wide_rows, axis=-1, keepdims=True) + norm_eps)
    return ((wide_rows * inverse * gain_row).astype(jnp.bfloat16), inverse)


def contract_trailing(left, right):
    return lax.dot_general(
        left, right, (((1,), (1,)), ((), ())), preferred_element_type=jnp.float32
    )


def contract_leading(left, right):
    return lax.dot_general(
        left, right, (((0,), (0,)), ((), ())), preferred_element_type=jnp.float32
    )


def section_parts(token_rows, gain_row, value_weight, tenant_adapters):
    value_down, value_up_factor, out_down, output_up_factor = tenant_adapters
    normalized_rows, inverse = normalize(token_rows, gain_row)
    lowrank_product = contract_trailing(normalized_rows, value_down).astype(jnp.bfloat16)
    value_blend = contract_trailing(normalized_rows, value_weight)
    value_blend = value_blend + adapter_scale * jnp.dot(
        lowrank_product, value_up_factor, preferred_element_type=jnp.float32
    )
    value_row_block = value_blend.astype(jnp.bfloat16)
    sidepath_rank = contract_trailing(value_row_block, out_down).astype(jnp.bfloat16)
    return (normalized_rows, inverse, lowrank_product, value_row_block, sidepath_rank)


def section_output(token_rows, layer_pieces, out_weight, tenant_adapters):
    blended_rows = token_rows.astype(jnp.float32) + jnp.dot(
        layer_pieces[3], out_weight, preferred_element_type=jnp.float32
    )
    blended_rows = blended_rows + adapter_scale * jnp.dot(
        layer_pieces[4], tenant_adapters[3], preferred_element_type=jnp.float32
    )
    return blended_rows.astype(jnp.bfloat16)


def section_backward(
    token_rows, input_gradient, layer_pieces, gain_row, value_weight, out_weight, tenant_adapters
):
    value_down, value_up_factor, out_down, output_up_factor = tenant_adapters
    normalized_rows, inverse, lowrank_product, value_row_block, sidepath_rank = layer_pieces
    sidepath_gradient = (
        adapter_scale * contract_trailing(input_gradient, output_up_factor)
    ).astype(jnp.bfloat16)
    value_gradient = contract_trailing(input_gradient, out_weight)
    value_gradient = (
        value_gradient + jnp.dot(sidepath_gradient, out_down, preferred_element_type=jnp.float32)
    ).astype(jnp.bfloat16)
    lowrank_gradient = (adapter_scale * contract_trailing(value_gradient, value_up_factor)).astype(
        jnp.bfloat16
    )
    grad_normed = jnp.dot(
        value_gradient, value_weight, preferred_element_type=jnp.float32
    ) + jnp.dot(lowrank_gradient, value_down, preferred_element_type=jnp.float32)
    scaled = grad_normed * gain_row
    wide_rows = token_rows.astype(jnp.float32)
    correction = jnp.mean(scaled * wide_rows, axis=-1, keepdims=True)
    grad_rows = inverse * scaled - wide_rows * (inverse * inverse * inverse) * correction
    grad_out = (input_gradient.astype(jnp.float32) + grad_rows).astype(jnp.bfloat16)
    gradient_pieces = (
        contract_leading(lowrank_gradient, normalized_rows),
        adapter_scale * contract_leading(lowrank_product, value_gradient),
        contract_leading(sidepath_gradient, value_row_block),
        adapter_scale * contract_leading(sidepath_rank, input_gradient),
    )
    return (grad_out, gradient_pieces)


def pass_section(token_rows, shift_by):
    return from_behind(token_rows, "pipe", shift_by)


def owner_layout(first, second, third, fourth):
    return (
        lax.all_to_all(first, "dp", split_axis=0, concat_axis=2, tiled=True),
        lax.all_to_all(second, "dp", split_axis=0, concat_axis=2, tiled=True),
        lax.all_to_all(third, "dp", split_axis=0, concat_axis=2, tiled=True),
        lax.all_to_all(fourth, "dp", split_axis=0, concat_axis=2, tiled=True),
    )


def pick_rows(picker, sliced_part):
    flat_rows = sliced_part.reshape(sliced_part.shape[0], -1)
    chosen = jnp.dot(picker, flat_rows, preferred_element_type=jnp.float32).astype(jnp.bfloat16)
    return chosen.reshape((picker.shape[0],) + sliced_part.shape[1:])


def sum_by_slot(slot_float, gathered_part):
    flat_rows = gathered_part.reshape(gathered_part.shape[0], -1)
    summed = lax.dot_general(
        slot_float,
        flat_rows,
        (((0,), (0,)), ((), ())),
        precision=lax.Precision.HIGHEST,
        preferred_element_type=jnp.float32,
    )
    return summed.astype(jnp.bfloat16).reshape((slot_float.shape[1],) + gathered_part.shape[1:])


def put_entry(stash, entry, micro_index, active):

    def update(stored_all, new_entry):
        previous = lax.dynamic_index_in_dim(stored_all, micro_index, 0, keepdims=False)
        return lax.dynamic_update_index_in_dim(
            stored_all, jnp.where(active, new_entry, previous), micro_index, 0
        )

    return jax.tree.map(update, stash, entry)


def get_entry(stash, micro_index):
    return jax.tree.map(
        lambda stored_all: lax.dynamic_index_in_dim(stored_all, micro_index, 0, keepdims=False),
        stash,
    )


def relay_body(
    inputs,
    cotangent,
    norm_gain,
    w_value,
    w_out,
    value_down,
    value_up_factor,
    out_down,
    output_up_factor,
    block_tenant,
    valid_tokens,
    tenant_slot,
):
    section_index = lax.axis_index("pipe")
    sections = lax.axis_size("pipe")
    member = lax.axis_index("dp")
    members = lax.axis_size("dp")
    queue_depth = inputs.shape[0]
    row_count = inputs.shape[1]
    micro_count = queue_depth * sections
    ticks = micro_count + sections - 1
    tenant_ids = jnp.arange(tenant_slot.shape[0], dtype=jnp.int32)
    tenant_hot = block_tenant[:, None] == tenant_ids[None, :]
    slot_of = jnp.sum(jnp.where(tenant_hot, tenant_slot[None, :], 0), axis=1)
    slot_hot = slot_of[:, None] == tenant_ids[None, :]
    member_hot = jnp.arange(members, dtype=jnp.int32) == member
    own_tenant = jnp.sum(jnp.where(member_hot, block_tenant, 0))
    own_valid = jnp.sum(jnp.where(member_hot, valid_tokens, 0))
    tenant_tokens = jnp.sum(jnp.where(block_tenant == own_tenant, valid_tokens, 0)).astype(
        jnp.float32
    )
    sliced = (
        lax.all_to_all(value_down[0], "dp", split_axis=2, concat_axis=0, tiled=True),
        lax.all_to_all(value_up_factor[0], "dp", split_axis=2, concat_axis=0, tiled=True),
        lax.all_to_all(out_down[0], "dp", split_axis=2, concat_axis=0, tiled=True),
        lax.all_to_all(output_up_factor[0], "dp", split_axis=2, concat_axis=0, tiled=True),
    )
    picker = slot_hot.astype(jnp.bfloat16)
    picked = [pick_rows(picker, sliced_part) for sliced_part in sliced]
    fetched = owner_layout(picked[0], picked[1], picked[2], picked[3])
    tenant_adapters = tuple((whole_part[0] for whole_part in fetched))
    gain_row = norm_gain[0]
    value_weight = w_value[0]
    out_weight = w_out[0]

    def token_weight(micro_index):
        position = micro_index * row_count + jnp.arange(row_count, dtype=jnp.int32)
        return (
            jnp.where(position < own_valid, 1.0, 0.0).astype(jnp.float32)[:, None] / tenant_tokens
        )

    def keep_entry(current):
        return (current,)

    def parts_of(entry):
        return section_parts(entry[0], gain_row, value_weight, tenant_adapters)

    blank = jnp.zeros((row_count, inputs.shape[2]), jnp.bfloat16)
    sample = keep_entry(blank)
    stash = jax.tree.map(
        lambda leaf_value: jnp.zeros((micro_count,) + leaf_value.shape, leaf_value.dtype), sample
    )
    accum = tuple((jnp.zeros(adapter_part.shape, jnp.float32) for adapter_part in tenant_adapters))

    def forward_tick(tick_index, arriving, feed_rows, stash_now, order):
        position = tick_index - section_index
        active = (position >= 0) & (position < micro_count)
        micro_index = order(jnp.clip(position, 0, micro_count - 1))
        current = jnp.where(section_index == 0, feed_rows, arriving)
        layer_pieces = section_parts(current, gain_row, value_weight, tenant_adapters)
        result = section_output(current, layer_pieces, out_weight, tenant_adapters)
        stash_now = put_entry(stash_now, keep_entry(current), micro_index, active)
        return (result, stash_now)

    def backward_tick(tick_index, arriving, feed_rows, stash_now, accum_now, order):
        position = tick_index - (sections - 1 - section_index)
        active = (position >= 0) & (position < micro_count)
        micro_index = order(jnp.clip(position, 0, micro_count - 1))
        entry = get_entry(stash_now, micro_index)
        seeded = (feed_rows.astype(jnp.float32) * token_weight(micro_index)).astype(jnp.bfloat16)
        input_gradient = jnp.where(section_index == sections - 1, seeded, arriving)
        grad_out, gradient_pieces = section_backward(
            entry[0],
            input_gradient,
            parts_of(entry),
            gain_row,
            value_weight,
            out_weight,
            tenant_adapters,
        )
        accum_now = tuple(
            (
                running + jnp.where(active, addend, 0.0)
                for running, addend in zip(accum_now, gradient_pieces)
            )
        )
        return (grad_out, accum_now)

    all_inputs, all_cotangents = (
        lax.all_gather(inputs, "pipe", axis=0, tiled=True),
        lax.all_gather(cotangent, "pipe", axis=0, tiled=True),
    )

    def plain_order(position):
        return position

    def forward_step(tick_index, carry):
        arriving, stash_now = carry
        feed_rows = lax.dynamic_index_in_dim(
            all_inputs, jnp.minimum(tick_index, micro_count - 1), 0, keepdims=False
        )
        result, stash_now = forward_tick(tick_index, arriving, feed_rows, stash_now, plain_order)
        return (pass_section(result, 1), stash_now)

    arriving, stash = lax.fori_loop(0, ticks, forward_step, (blank, stash))

    def backward_step(tick_index, carry):
        arriving, accum_now = carry
        feed_rows = lax.dynamic_index_in_dim(
            all_cotangents, jnp.minimum(tick_index, micro_count - 1), 0, keepdims=False
        )
        grad_out, accum_now = backward_tick(
            tick_index, arriving, feed_rows, stash, accum_now, plain_order
        )
        return (pass_section(grad_out, sections - 1), accum_now)

    arriving, accum = lax.fori_loop(0, ticks, backward_step, (blank, accum))
    spread = (
        lax.all_to_all(
            accum[0][None].astype(jnp.bfloat16), "dp", split_axis=2, concat_axis=0, tiled=True
        ).astype(jnp.float32),
        lax.all_to_all(
            accum[1][None].astype(jnp.bfloat16), "dp", split_axis=2, concat_axis=0, tiled=True
        ).astype(jnp.float32),
        lax.all_to_all(
            accum[2][None].astype(jnp.bfloat16), "dp", split_axis=2, concat_axis=0, tiled=True
        ).astype(jnp.float32),
        lax.all_to_all(
            accum[3][None].astype(jnp.bfloat16), "dp", split_axis=2, concat_axis=0, tiled=True
        ).astype(jnp.float32),
    )
    slot_float = slot_hot.astype(jnp.float32)
    totals = [sum_by_slot(slot_float, gathered_part) for gathered_part in spread]
    owned = owner_layout(totals[0], totals[1], totals[2], totals[3])
    return (owned[0][None], owned[1][None], owned[2][None], owned[3][None])


def trail(left, right):
    return lax.dot_general(
        left, right, (((1,), (1,)), ((), ())), preferred_element_type=jnp.float32
    )


def plain(left, right):
    return jnp.dot(left, right, preferred_element_type=jnp.float32)


def row_weights(block_tenant, valid_tokens, tenant_slot, member, micro_count, row_count):
    tenant_ids = jnp.arange(tenant_slot.shape[0], dtype=jnp.int32)
    tenant_hot = block_tenant[:, None] == tenant_ids[None, :]
    slot_of = jnp.sum(jnp.where(tenant_hot, tenant_slot[None, :], 0), axis=1)
    same = block_tenant[:, None] == block_tenant[None, :]
    tokens = jnp.sum(jnp.where(same, valid_tokens[None, :], 0), axis=1).astype(jnp.float32)
    position = jnp.arange(micro_count * row_count, dtype=jnp.int32)
    keep = (position[None, :] < valid_tokens[:, None]) & (slot_of[:, None] == member)
    return jnp.where(keep, 1.0, 0.0).astype(jnp.float32) / tokens[:, None]


def forward_small(projection, inverse, up_turned, out_down):
    hd = projection.shape[0] - out_down.shape[0]
    scaled = projection * inverse
    lowrank = scaled[hd:].astype(jnp.bfloat16)
    value = (scaled[:hd] + adapter_scale * plain(up_turned, lowrank)).astype(jnp.bfloat16)
    side = plain(out_down, value).astype(jnp.bfloat16)
    return lowrank, value, side


def backward_small(back, up_factor, down_turned):
    hd = up_factor.shape[1]
    grad_side = (adapter_scale * back[hd:]).astype(jnp.bfloat16)
    grad_value = (back[:hd] + plain(down_turned, grad_side)).astype(jnp.bfloat16)
    grad_low = (adapter_scale * plain(up_factor, grad_value)).astype(jnp.bfloat16)
    return grad_side, grad_value, grad_low


def columns_body(
    inputs,
    cotangent,
    norm_gain,
    w_value,
    w_out,
    value_down,
    value_up_factor,
    out_down,
    output_up_factor,
    block_tenant,
    valid_tokens,
    tenant_slot,
):
    section = lax.axis_index("pipe")
    sections = lax.axis_size("pipe")
    member = lax.axis_index("dp")
    row_count, width = inputs.shape[1:]
    micro_count = inputs.shape[0] * sections
    gain = norm_gain[0][None]
    into = jnp.concatenate([w_value[0], value_down[0, 0]]).astype(jnp.float32) * gain
    into = into.astype(jnp.bfloat16)
    outof = jnp.concatenate([w_out[0], output_up_factor[0, 0]])
    weights = lax.all_to_all(
        jnp.stack([into, outof])[None], "pipe", split_axis=3, concat_axis=0, tiled=True
    )
    factors = lax.all_gather(
        jnp.stack([value_up_factor[0, 0], out_down[0, 0]]), "pipe", axis=0
    )
    tokens = lax.all_to_all(
        jnp.stack([inputs, cotangent], axis=1), "pipe", split_axis=3, concat_axis=0, tiled=True
    )
    tokens = lax.all_gather(tokens, "dp", axis=0)
    columns = tokens.shape[-1]
    rows = tokens[:, :, 0].reshape(-1, columns)
    weight = row_weights(
        block_tenant, valid_tokens, tenant_slot, member, micro_count, row_count
    ).reshape(-1, 1)
    gradient = (tokens[:, :, 1].reshape(-1, columns).astype(jnp.float32) * weight).astype(
        jnp.bfloat16
    )
    kept = []
    for layer in range(sections):
        wide = rows.astype(jnp.float32)
        squares = jnp.sum(wide * wide, axis=1)[None]
        partial = jnp.concatenate([trail(weights[layer, 0], rows), squares])
        whole = lax.psum(partial, "pipe")
        projection = whole[:-1]
        inverse = lax.rsqrt(whole[-1:] / width + norm_eps)
        lowrank, value, side = forward_small(
            projection, inverse, factors[layer, 0].T, factors[layer, 1]
        )
        kept.append((rows, projection, inverse, lowrank, value, side))
        if layer < sections - 1:
            mixed = jnp.concatenate([value, adapter_scale * side])
            rows = (wide + contract_leading(mixed, weights[layer, 1])).astype(jnp.bfloat16)
    downs, ups, small_ups, small_downs = [], [], [], []
    for layer in reversed(range(sections)):
        rows, projection, inverse, lowrank, value, side = kept[layer]
        back = lax.psum(trail(weights[layer, 1], gradient), "pipe")
        grad_side, grad_value, grad_low = backward_small(
            back, factors[layer, 0], factors[layer, 1].T
        )
        both = jnp.concatenate([grad_value, grad_low]).astype(jnp.float32)
        correction = jnp.sum(both * projection, axis=0, keepdims=True) / width
        scaled = (both * inverse).astype(jnp.bfloat16)
        downs.append(plain(scaled[value.shape[0] :], rows).astype(jnp.bfloat16))
        ups.append((adapter_scale * plain(side, gradient)).astype(jnp.bfloat16))
        small_ups.append((adapter_scale * trail(lowrank, grad_value)).astype(jnp.bfloat16))
        small_downs.append(trail(grad_side, value).astype(jnp.bfloat16))
        if layer > 0:
            shrink = (inverse * inverse * inverse * correction).reshape(-1, 1)
            gradient = (
                gradient.astype(jnp.float32)
                + contract_leading(scaled, weights[layer, 0])
                - rows.astype(jnp.float32) * shrink
            ).astype(jnp.bfloat16)
    wide_pair = jnp.stack([jnp.stack(downs[::-1]), jnp.stack(ups[::-1])], axis=1)
    wide_pair = lax.all_to_all(wide_pair, "pipe", split_axis=0, concat_axis=3, tiled=True)[0]
    value_down_grad = (wide_pair[0].astype(jnp.float32) * gain).astype(jnp.bfloat16)
    own_up = lax.dynamic_index_in_dim(jnp.stack(small_ups[::-1]), section, 0, keepdims=False)
    own_down = lax.dynamic_index_in_dim(jnp.stack(small_downs[::-1]), section, 0, keepdims=False)
    return (
        value_down_grad[None, None],
        own_up[None, None],
        own_down[None, None],
        wide_pair[1][None, None],
    )


def solution(mesh):
    sections = mesh.shape["pipe"]

    def run(*arrays):
        depth, row_total, width = arrays[0].shape
        kept_bytes = 2 * depth * row_total * (width // sections) * sections
        chosen = columns_body if kept_bytes <= stash_limit else relay_body
        return place(chosen)(*arrays)

    def place(chosen):
        return jax.shard_map(
            chosen,
            mesh=mesh,
            in_specs=(
                P("pipe", "dp", None),
                P("pipe", "dp", None),
                P("pipe", None),
                P("pipe", None, None),
                P("pipe", None, None),
                P("pipe", "dp", None, None),
                P("pipe", "dp", None, None),
                P("pipe", "dp", None, None),
                P("pipe", "dp", None, None),
                P(),
                P(),
                P(),
            ),
            out_specs=(
                P("pipe", "dp", None, None),
                P("pipe", "dp", None, None),
                P("pipe", "dp", None, None),
                P("pipe", "dp", None, None),
            ),
            check_vma=False,
        )

    return run
```

```python
import functools

import jax
import jax.numpy as jnp
from jax import lax
from jax.experimental import pallas as pl
from jax.experimental.pallas import tpu as pltpu
from jax.sharding import PartitionSpec as P

adapter_scale = 2.0
norm_eps = 1e-05
stash_limit = 8 * 2**20


def from_behind(value, axis, by):
    peers = lax.axis_size(axis)
    return lax.ppermute(value, axis, [(i, (i + by) % peers) for i in range(peers)])


def normalize(token_rows, gain_row):
    wide_rows = token_rows.astype(jnp.float32)
    inverse = lax.rsqrt(jnp.mean(wide_rows * wide_rows, axis=-1, keepdims=True) + norm_eps)
    return ((wide_rows * inverse * gain_row).astype(jnp.bfloat16), inverse)


def contract_trailing(left, right):
    return lax.dot_general(
        left, right, (((1,), (1,)), ((), ())), preferred_element_type=jnp.float32
    )


def contract_leading(left, right):
    return lax.dot_general(
        left, right, (((0,), (0,)), ((), ())), preferred_element_type=jnp.float32
    )


def section_parts(token_rows, gain_row, value_weight, tenant_adapters):
    value_down, value_up_factor, out_down, output_up_factor = tenant_adapters
    normalized_rows, inverse = normalize(token_rows, gain_row)
    lowrank_product = contract_trailing(normalized_rows, value_down).astype(jnp.bfloat16)
    value_blend = contract_trailing(normalized_rows, value_weight)
    value_blend = value_blend + adapter_scale * jnp.dot(
        lowrank_product, value_up_factor, preferred_element_type=jnp.float32
    )
    value_row_block = value_blend.astype(jnp.bfloat16)
    sidepath_rank = contract_trailing(value_row_block, out_down).astype(jnp.bfloat16)
    return (normalized_rows, inverse, lowrank_product, value_row_block, sidepath_rank)


def section_output(token_rows, layer_pieces, out_weight, tenant_adapters):
    blended_rows = token_rows.astype(jnp.float32) + jnp.dot(
        layer_pieces[3], out_weight, preferred_element_type=jnp.float32
    )
    blended_rows = blended_rows + adapter_scale * jnp.dot(
        layer_pieces[4], tenant_adapters[3], preferred_element_type=jnp.float32
    )
    return blended_rows.astype(jnp.bfloat16)


def section_backward(
    token_rows, input_gradient, layer_pieces, gain_row, value_weight, out_weight, tenant_adapters
):
    value_down, value_up_factor, out_down, output_up_factor = tenant_adapters
    normalized_rows, inverse, lowrank_product, value_row_block, sidepath_rank = layer_pieces
    sidepath_gradient = (
        adapter_scale * contract_trailing(input_gradient, output_up_factor)
    ).astype(jnp.bfloat16)
    value_gradient = contract_trailing(input_gradient, out_weight)
    value_gradient = (
        value_gradient + jnp.dot(sidepath_gradient, out_down, preferred_element_type=jnp.float32)
    ).astype(jnp.bfloat16)
    lowrank_gradient = (adapter_scale * contract_trailing(value_gradient, value_up_factor)).astype(
        jnp.bfloat16
    )
    grad_normed = jnp.dot(
        value_gradient, value_weight, preferred_element_type=jnp.float32
    ) + jnp.dot(lowrank_gradient, value_down, preferred_element_type=jnp.float32)
    scaled = grad_normed * gain_row
    wide_rows = token_rows.astype(jnp.float32)
    correction = jnp.mean(scaled * wide_rows, axis=-1, keepdims=True)
    grad_rows = inverse * scaled - wide_rows * (inverse * inverse * inverse) * correction
    grad_out = (input_gradient.astype(jnp.float32) + grad_rows).astype(jnp.bfloat16)
    gradient_pieces = (
        contract_leading(lowrank_gradient, normalized_rows),
        adapter_scale * contract_leading(lowrank_product, value_gradient),
        contract_leading(sidepath_gradient, value_row_block),
        adapter_scale * contract_leading(sidepath_rank, input_gradient),
    )
    return (grad_out, gradient_pieces)


def pass_section(token_rows, shift_by):
    return from_behind(token_rows, "pipe", shift_by)


def owner_layout(first, second, third, fourth):
    return (
        lax.all_to_all(first, "dp", split_axis=0, concat_axis=2, tiled=True),
        lax.all_to_all(second, "dp", split_axis=0, concat_axis=2, tiled=True),
        lax.all_to_all(third, "dp", split_axis=0, concat_axis=2, tiled=True),
        lax.all_to_all(fourth, "dp", split_axis=0, concat_axis=2, tiled=True),
    )


def pick_rows(picker, sliced_part):
    flat_rows = sliced_part.reshape(sliced_part.shape[0], -1)
    chosen = jnp.dot(picker, flat_rows, preferred_element_type=jnp.float32).astype(jnp.bfloat16)
    return chosen.reshape((picker.shape[0],) + sliced_part.shape[1:])


def sum_by_slot(slot_float, gathered_part):
    flat_rows = gathered_part.reshape(gathered_part.shape[0], -1)
    summed = lax.dot_general(
        slot_float,
        flat_rows,
        (((0,), (0,)), ((), ())),
        precision=lax.Precision.HIGHEST,
        preferred_element_type=jnp.float32,
    )
    return summed.astype(jnp.bfloat16).reshape((slot_float.shape[1],) + gathered_part.shape[1:])


def put_entry(stash, entry, micro_index, active):

    def update(stored_all, new_entry):
        previous = lax.dynamic_index_in_dim(stored_all, micro_index, 0, keepdims=False)
        return lax.dynamic_update_index_in_dim(
            stored_all, jnp.where(active, new_entry, previous), micro_index, 0
        )

    return jax.tree.map(update, stash, entry)


def get_entry(stash, micro_index):
    return jax.tree.map(
        lambda stored_all: lax.dynamic_index_in_dim(stored_all, micro_index, 0, keepdims=False),
        stash,
    )


def relay_body(
    inputs,
    cotangent,
    norm_gain,
    w_value,
    w_out,
    value_down,
    value_up_factor,
    out_down,
    output_up_factor,
    block_tenant,
    valid_tokens,
    tenant_slot,
):
    section_index = lax.axis_index("pipe")
    sections = lax.axis_size("pipe")
    member = lax.axis_index("dp")
    members = lax.axis_size("dp")
    queue_depth = inputs.shape[0]
    row_count = inputs.shape[1]
    micro_count = queue_depth * sections
    ticks = micro_count + sections - 1
    tenant_ids = jnp.arange(tenant_slot.shape[0], dtype=jnp.int32)
    tenant_hot = block_tenant[:, None] == tenant_ids[None, :]
    slot_of = jnp.sum(jnp.where(tenant_hot, tenant_slot[None, :], 0), axis=1)
    slot_hot = slot_of[:, None] == tenant_ids[None, :]
    member_hot = jnp.arange(members, dtype=jnp.int32) == member
    own_tenant = jnp.sum(jnp.where(member_hot, block_tenant, 0))
    own_valid = jnp.sum(jnp.where(member_hot, valid_tokens, 0))
    tenant_tokens = jnp.sum(jnp.where(block_tenant == own_tenant, valid_tokens, 0)).astype(
        jnp.float32
    )
    sliced = (
        lax.all_to_all(value_down[0], "dp", split_axis=2, concat_axis=0, tiled=True),
        lax.all_to_all(value_up_factor[0], "dp", split_axis=2, concat_axis=0, tiled=True),
        lax.all_to_all(out_down[0], "dp", split_axis=2, concat_axis=0, tiled=True),
        lax.all_to_all(output_up_factor[0], "dp", split_axis=2, concat_axis=0, tiled=True),
    )
    picker = slot_hot.astype(jnp.bfloat16)
    picked = [pick_rows(picker, sliced_part) for sliced_part in sliced]
    fetched = owner_layout(picked[0], picked[1], picked[2], picked[3])
    tenant_adapters = tuple((whole_part[0] for whole_part in fetched))
    gain_row = norm_gain[0]
    value_weight = w_value[0]
    out_weight = w_out[0]

    def token_weight(micro_index):
        position = micro_index * row_count + jnp.arange(row_count, dtype=jnp.int32)
        return (
            jnp.where(position < own_valid, 1.0, 0.0).astype(jnp.float32)[:, None] / tenant_tokens
        )

    def keep_entry(current):
        return (current,)

    def parts_of(entry):
        return section_parts(entry[0], gain_row, value_weight, tenant_adapters)

    blank = jnp.zeros((row_count, inputs.shape[2]), jnp.bfloat16)
    sample = keep_entry(blank)
    stash = jax.tree.map(
        lambda leaf_value: jnp.zeros((micro_count,) + leaf_value.shape, leaf_value.dtype), sample
    )
    accum = tuple((jnp.zeros(adapter_part.shape, jnp.float32) for adapter_part in tenant_adapters))

    def forward_tick(tick_index, arriving, feed_rows, stash_now, order):
        position = tick_index - section_index
        active = (position >= 0) & (position < micro_count)
        micro_index = order(jnp.clip(position, 0, micro_count - 1))
        current = jnp.where(section_index == 0, feed_rows, arriving)
        layer_pieces = section_parts(current, gain_row, value_weight, tenant_adapters)
        result = section_output(current, layer_pieces, out_weight, tenant_adapters)
        stash_now = put_entry(stash_now, keep_entry(current), micro_index, active)
        return (result, stash_now)

    def backward_tick(tick_index, arriving, feed_rows, stash_now, accum_now, order):
        position = tick_index - (sections - 1 - section_index)
        active = (position >= 0) & (position < micro_count)
        micro_index = order(jnp.clip(position, 0, micro_count - 1))
        entry = get_entry(stash_now, micro_index)
        seeded = (feed_rows.astype(jnp.float32) * token_weight(micro_index)).astype(jnp.bfloat16)
        input_gradient = jnp.where(section_index == sections - 1, seeded, arriving)
        grad_out, gradient_pieces = section_backward(
            entry[0],
            input_gradient,
            parts_of(entry),
            gain_row,
            value_weight,
            out_weight,
            tenant_adapters,
        )
        accum_now = tuple(
            (
                running + jnp.where(active, addend, 0.0)
                for running, addend in zip(accum_now, gradient_pieces)
            )
        )
        return (grad_out, accum_now)

    all_inputs, all_cotangents = (
        lax.all_gather(inputs, "pipe", axis=0, tiled=True),
        lax.all_gather(cotangent, "pipe", axis=0, tiled=True),
    )

    def plain_order(position):
        return position

    def forward_step(tick_index, carry):
        arriving, stash_now = carry
        feed_rows = lax.dynamic_index_in_dim(
            all_inputs, jnp.minimum(tick_index, micro_count - 1), 0, keepdims=False
        )
        result, stash_now = forward_tick(tick_index, arriving, feed_rows, stash_now, plain_order)
        return (pass_section(result, 1), stash_now)

    arriving, stash = lax.fori_loop(0, ticks, forward_step, (blank, stash))

    def backward_step(tick_index, carry):
        arriving, accum_now = carry
        feed_rows = lax.dynamic_index_in_dim(
            all_cotangents, jnp.minimum(tick_index, micro_count - 1), 0, keepdims=False
        )
        grad_out, accum_now = backward_tick(
            tick_index, arriving, feed_rows, stash, accum_now, plain_order
        )
        return (pass_section(grad_out, sections - 1), accum_now)

    arriving, accum = lax.fori_loop(0, ticks, backward_step, (blank, accum))
    spread = (
        lax.all_to_all(
            accum[0][None].astype(jnp.bfloat16), "dp", split_axis=2, concat_axis=0, tiled=True
        ).astype(jnp.float32),
        lax.all_to_all(
            accum[1][None].astype(jnp.bfloat16), "dp", split_axis=2, concat_axis=0, tiled=True
        ).astype(jnp.float32),
        lax.all_to_all(
            accum[2][None].astype(jnp.bfloat16), "dp", split_axis=2, concat_axis=0, tiled=True
        ).astype(jnp.float32),
        lax.all_to_all(
            accum[3][None].astype(jnp.bfloat16), "dp", split_axis=2, concat_axis=0, tiled=True
        ).astype(jnp.float32),
    )
    slot_float = slot_hot.astype(jnp.float32)
    totals = [sum_by_slot(slot_float, gathered_part) for gathered_part in spread]
    owned = owner_layout(totals[0], totals[1], totals[2], totals[3])
    return (owned[0][None], owned[1][None], owned[2][None], owned[3][None])


def trail(left, right):
    return lax.dot_general(
        left, right, (((1,), (1,)), ((), ())), preferred_element_type=jnp.float32
    )


def plain(left, right):
    return jnp.dot(left, right, preferred_element_type=jnp.float32)


def row_weights(block_tenant, valid_tokens, tenant_slot, member, micro_count, row_count):
    tenant_ids = jnp.arange(tenant_slot.shape[0], dtype=jnp.int32)
    tenant_hot = block_tenant[:, None] == tenant_ids[None, :]
    slot_of = jnp.sum(jnp.where(tenant_hot, tenant_slot[None, :], 0), axis=1)
    same = block_tenant[:, None] == block_tenant[None, :]
    tokens = jnp.sum(jnp.where(same, valid_tokens[None, :], 0), axis=1).astype(jnp.float32)
    position = jnp.arange(micro_count * row_count, dtype=jnp.int32)
    keep = (position[None, :] < valid_tokens[:, None]) & (slot_of[:, None] == member)
    return jnp.where(keep, 1.0, 0.0).astype(jnp.float32) / tokens[:, None]


def columns_kernel(
    shape,
    tok,
    wts,
    fac,
    row_weight,
    gain,
    out_vd,
    out_vu,
    out_od,
    out_ou,
    hid,
    grad,
    cot,
    tbuf,
    pbuf,
    qbuf,
    fbuf,
    turned,
    land,
    mine,
    fx_out,
    fx_in,
    bx_out,
    bx_in,
    local_sem,
    tok_sem,
    fac_sem,
    p_sem,
    q_sem,
    psib_sem,
    qsib_sem,
    x_up,
    x_down,
    x_sib,
    c_up,
    c_down,
    c_sib,
    fx_sem,
    bx_sem,
    land_sem,
):
    sections, members = shape
    levels = members // 2
    section, member = lax.axis_index("pipe"), lax.axis_index("dp")
    core, level = lax.rem(member, 2), lax.div(member, 2)
    sibling = (section, member + 1 - 2 * core)
    row_total, columns = hid.shape[1:]
    block = row_total // members
    width = columns * sections
    hd, rank = wts.shape[0] // 2 - out_vu.shape[0], out_vu.shape[0]
    half, ranks = hd // 2, wts.shape[0] // 2
    peers = [lax.rem(section + j, sections) for j in range(1, sections)]
    step = min(512, columns)
    chunks = columns // step

    def remote(src, dst, sem, slot, target, got=None):
        return pltpu.make_async_remote_copy(
            src_ref=src,
            dst_ref=dst,
            send_sem=sem.at[0, slot],
            recv_sem=sem.at[1, slot if got is None else got],
            device_id=target,
            device_id_type=pl.DeviceIdType.MESH,
        )

    barrier = pltpu.get_barrier_semaphore()
    greeted = [(q, member) for q in peers] + [sibling]
    greeted += [(section, lax.rem(member + by, members)) for by in (2, members - 2)]
    for target in greeted:
        pl.semaphore_signal(
            barrier, inc=1, device_id=target, device_id_type=pl.DeviceIdType.MESH
        )
    own_columns = pl.ds(pl.multiple_of(section * columns, columns), columns)
    local = [
        pltpu.make_async_copy(tok.at[:, own_columns], tbuf.at[section], local_sem.at[0]),
        pltpu.make_async_copy(fac, fbuf.at[section], local_sem.at[1]),
        pltpu.make_async_copy(
            wts.at[pl.ds(0, ranks), own_columns], pbuf.at[section], local_sem.at[2]
        ),
        pltpu.make_async_copy(
            wts.at[pl.ds(ranks, ranks), own_columns], qbuf.at[section], local_sem.at[3]
        ),
    ]
    for copy in local:
        copy.start()
    pl.semaphore_wait(barrier, len(greeted))

    share = half + rank
    share_rows = pl.ds(pl.multiple_of(core * half, 16), share)
    out_rows = pl.ds(pl.multiple_of(ranks + core * half, 16), share)
    pass_rows = pl.ds(pl.multiple_of(core * share, 16), half)

    def to_columns(q):
        return pl.ds(pl.multiple_of(q * columns, columns), columns)

    def tok_copy(j, src_section):
        q = peers[j]
        return remote(
            tok.at[:, to_columns(q)], tbuf.at[src_section], tok_sem, j, (q, member), src_section
        )

    def fac_copy(j, src_section):
        return remote(fac, fbuf.at[src_section], fac_sem, j, (peers[j], member), src_section)

    def p_copy(j, src_section):
        q = peers[j]
        return remote(
            wts.at[share_rows, to_columns(q)],
            pbuf.at[src_section, share_rows],
            p_sem,
            j,
            (q, member),
            src_section,
        )

    def q_copy(j, src_section):
        q = peers[j]
        return remote(
            wts.at[out_rows, to_columns(q)],
            qbuf.at[src_section, share_rows],
            q_sem,
            j,
            (q, member),
            src_section,
        )

    def sib_weight(buf, sem, layer):
        piece = buf.at[layer, pass_rows]
        return remote(piece, piece, sem, layer, sibling)

    def arrive(copy_of, layer):
        @pl.when(section != layer)
        def _():
            copy_of(0, layer).wait_recv()

    def arrive_and_pass(copy_of, buf, sem, layer):
        @pl.when(section != layer)
        def _():
            copy_of(0, layer).wait_recv()
            sib_weight(buf, sem, layer).start()

    def passed(buf, sem, layer):
        @pl.when(section != layer)
        def _():
            sib_weight(buf, sem, layer).wait_recv()

    def block_rows(buf, at_level):
        start = pl.multiple_of((at_level * 2 + core) * block, block)
        return buf.at[pl.ds(start, block)]

    def up_copy(buf, sem, k):
        piece = block_rows(buf, level - k)
        return remote(piece, piece, sem, k, (section, member + 2))

    def down_copy(buf, sem, k):
        piece = block_rows(buf, level + k)
        return remote(piece, piece, sem, k, (section, member - 2))

    def sib_copy(buf, sem, at_level):
        piece = block_rows(buf, at_level)
        return remote(piece, piece, sem, at_level, sibling)

    def line_start(buf, up, down, k):
        @pl.when((level < levels - 1) & (level - k >= 0))
        def _():
            up_copy(buf, up, k).start()

        @pl.when((level > 0) & (level + k < levels))
        def _():
            down_copy(buf, down, k).start()

    def line_arrive(buf, up, down, sib, k):
        @pl.when(level - 1 - k >= 0)
        def _():
            up_copy(buf, up, k).wait_recv()

        @pl.when(level + 1 + k < levels)
        def _():
            down_copy(buf, down, k).wait_recv()

        if k + 1 < levels - 1:
            line_start(buf, up, down, k + 1)

        @pl.when(level - 1 - k >= 0)
        def _():
            sib_copy(buf, sib, level - 1 - k).start()

        @pl.when(level + 1 + k < levels)
        def _():
            sib_copy(buf, sib, level + 1 + k).start()

    def line_sent(buf, up, down, sib):
        for k in range(levels - 1):

            @pl.when((level < levels - 1) & (level - k >= 0))
            def _(k=k):
                up_copy(buf, up, k).wait_send()

            @pl.when((level > 0) & (level + k < levels))
            def _(k=k):
                down_copy(buf, down, k).wait_send()

        for at_level in range(levels):
            sib_copy(buf, sib, at_level).wait_send()

    def sum_copy(out, into, sem, layer, j):
        return remote(
            out.at[layer],
            into.at[layer, j],
            sem,
            layer * (sections - 1) + j,
            (peers[j], member),
        )

    def send_sum(out, into, sem, layer, partial):
        out[layer] = partial.astype(jnp.bfloat16)
        for j in range(sections - 1):
            sum_copy(out, into, sem, layer, j).start()

    def whole_sum(out, into, sem, layer, partial):
        for j in range(sections - 1):
            sum_copy(out, into, sem, layer, j).wait_recv()
        for j in range(sections - 1):
            partial = partial + into[layer, j].astype(jnp.float32)
        return partial

    for j in range(sections - 1):
        tok_copy(j, section).start()
    for j in range(sections - 1):
        p_copy(j, section).start()
    for j in range(sections - 1):
        fac_copy(j, section).start()

    local[0].wait()
    for layer in range(sections):
        arrive(tok_copy, layer)
    per = block // sections
    for t in range(chunks):
        at = pl.ds(t * step, step)
        wide = [tbuf[m, :, at].astype(jnp.float32) for m in range(sections)]
        own = pl.ds(pl.multiple_of(member * block, block), block)
        hid[0, own, at] = jnp.concatenate([w[:per] for w in wide]).astype(jnp.bfloat16)
        cot[own, at] = jnp.concatenate([w[per:] for w in wide]).astype(jnp.bfloat16)
    x0 = hid.at[0]
    line_start(x0, x_up, x_down, 0)
    sib_copy(x0, x_sib, level).start()
    for j in range(sections - 1):
        q_copy(j, section).start()
    for k in range(levels - 1):
        line_arrive(x0, x_up, x_down, x_sib, k)
    line_start(cot, c_up, c_down, 0)
    sib_copy(cot, c_sib, level).start()
    for copy in local[1:]:
        copy.wait()
    for layer in range(sections):
        arrive_and_pass(p_copy, pbuf, psib_sem, layer)
        arrive(fac_copy, layer)
    for at_level in range(levels):
        sib_copy(x0, x_sib, at_level).wait_recv()

    ones = jnp.ones((16, step), jnp.bfloat16)

    def chunk(t):
        return pl.ds(pl.multiple_of(t * step, step), step)

    def project(layer, at, rows):
        squares = (rows.astype(jnp.float32) * rows.astype(jnp.float32)).astype(jnp.bfloat16)
        return trail(pbuf[layer, :, at], rows), trail(ones, squares)

    def add(left, right):
        return tuple(a + b for a, b in zip(left, right))

    zero_sum = (
        jnp.zeros((ranks, row_total), jnp.float32),
        jnp.zeros((16, row_total), jnp.float32),
    )

    def turn(parts):
        parts = jnp.concatenate(parts)
        spare = jnp.zeros((128 - parts.shape[0], row_total), jnp.float32)
        return jnp.concatenate([parts, spare]).T

    def first(t, total):
        return add(total, project(0, chunk(t), hid[0, :, chunk(t)]))

    passed(pbuf, psib_sem, 0)
    total = lax.fori_loop(0, chunks, first, zero_sum)
    kept = []
    last = sections - 1
    back = None
    for layer in range(sections):
        squares = total[1][:8]
        high = squares.astype(jnp.bfloat16).astype(jnp.float32)
        partial = jnp.concatenate([total[0], high, squares - high])
        send_sum(fx_out, fx_in, fx_sem, layer, partial)
        if layer < levels - 1:
            line_arrive(cot, c_up, c_down, c_sib, layer)
        if layer == 0:
            arrive_and_pass(q_copy, qbuf, qsib_sem, 0)
            passed(qbuf, qsib_sem, 0)
        if layer == 1:
            for later in range(1, sections):
                arrive_and_pass(q_copy, qbuf, qsib_sem, later)
        if 0 < layer:
            passed(qbuf, qsib_sem, layer)
        if layer < last:
            passed(pbuf, psib_sem, layer + 1)
        if layer == last:
            for k in range(last + 1, levels - 1):
                line_arrive(cot, c_up, c_down, c_sib, k)
            for at_level in range(levels):
                sib_copy(cot, c_sib, at_level).wait_recv()

            def seed(t, total_now):
                at = chunk(t)
                top = (cot[:, at].astype(jnp.float32) * row_weight[...]).astype(jnp.bfloat16)
                grad[last, :, at] = top
                return total_now + trail(qbuf[last, :, at], top)

            back = lax.fori_loop(0, chunks, seed, zero_sum[0])
            send_sum(bx_out, bx_in, bx_sem, last, back)
        whole = whole_sum(fx_out, fx_in, fx_sem, layer, partial)
        projection = whole[:ranks]
        inverse = lax.rsqrt((whole[ranks : ranks + 1] + whole[ranks + 8 : ranks + 9]) / width + norm_eps)
        factor = fbuf[layer]
        scaled = projection * inverse
        lowrank = scaled[half : half + rank].astype(jnp.bfloat16)
        straight = jnp.concatenate([scaled[:half], scaled[half + rank :]])
        value = (
            straight + adapter_scale * plain(factor[rank:, :rank], lowrank)
        ).astype(jnp.bfloat16)
        side = plain(factor[:rank, hd : 2 * hd], value).astype(jnp.bfloat16)
        kept.append((projection, inverse, lowrank, value, side))
        if layer < last:
            wide_value = value.astype(jnp.float32)
            mixed = [
                wide_value[:half],
                adapter_scale * side.astype(jnp.float32),
                wide_value[half:],
            ]
            turned[...] = turn(mixed).astype(jnp.bfloat16)

            def update(t, total_now, layer=layer):
                at = chunk(t)
                rows = hid[layer, :, at].astype(jnp.float32)
                rows = rows + plain(turned[:, :ranks], qbuf[layer, :, at])
                rows = rows.astype(jnp.bfloat16)
                hid[layer + 1, :, at] = rows
                return add(total_now, project(layer + 1, at, rows))

            total = lax.fori_loop(0, chunks, update, zero_sum)

    for layer in reversed(range(sections)):
        projection, inverse, lowrank, value, side = kept[layer]
        factor = fbuf[layer]
        whole = whole_sum(bx_out, bx_in, bx_sem, layer, back)
        grad_side = (adapter_scale * whole[half : half + rank]).astype(jnp.bfloat16)
        straight = jnp.concatenate([whole[:half], whole[half + rank :]])
        grad_value = (straight + plain(factor[rank:, hd : hd + rank], grad_side)).astype(
            jnp.bfloat16
        )
        grad_low = (adapter_scale * plain(factor[:rank, :hd], grad_value)).astype(jnp.bfloat16)
        wide_value = grad_value.astype(jnp.float32)
        both = jnp.concatenate(
            [wide_value[:half], grad_low.astype(jnp.float32), wide_value[half:]]
        )
        scaled = both * inverse
        if layer > 0:
            correction = jnp.sum(both * projection, axis=0, keepdims=True) / width
            shrink = inverse * inverse * inverse * correction
            shrink = jnp.broadcast_to(shrink, (8, row_total))
            columns_of = turn([scaled, shrink])
            turned[...] = columns_of.astype(jnp.bfloat16)
            shrink_column = columns_of[:, ranks : ranks + 1]

            def step_back(t, total_now, layer=layer, shrink_column=shrink_column):
                at = chunk(t)
                rows = hid[layer, :, at].astype(jnp.float32)
                fresh = grad[layer, :, at].astype(jnp.float32)
                fresh = fresh + plain(turned[:, :ranks], pbuf[layer, :, at])
                fresh = (fresh - rows * shrink_column).astype(jnp.bfloat16)
                grad[layer - 1, :, at] = fresh
                return total_now + trail(qbuf[layer - 1, :, at], fresh)

            back = lax.fori_loop(0, chunks, step_back, zero_sum[0])
            send_sum(bx_out, bx_in, bx_sem, layer - 1, back)
        low_scaled = scaled[half : half + rank].astype(jnp.bfloat16)

        def gather(t, carry, layer=layer, low_scaled=low_scaled, side=side):
            at = chunk(t)
            mine[layer, 0, :, at] = plain(low_scaled, hid[layer, :, at]).astype(jnp.bfloat16)
            mine[layer, 1, :, at] = (
                adapter_scale * plain(side, grad[layer, :, at])
            ).astype(jnp.bfloat16)
            return carry

        lax.fori_loop(0, chunks, gather, 0)
        land_copy = remote(
            mine.at[layer], land.at[section], land_sem, layer, (layer, member), section
        )

        @pl.when(section != layer)
        def _(land_copy=land_copy):
            land_copy.start()

        @pl.when(section == layer)
        def _(layer=layer, lowrank=lowrank, grad_value=grad_value, grad_side=grad_side, value=value):
            land[layer] = mine[layer]
            out_vu[...] = (adapter_scale * trail(lowrank, grad_value)).astype(jnp.bfloat16)
            out_od[...] = trail(grad_side, value).astype(jnp.bfloat16)

    for source in range(sections):

        @pl.when(section != source)
        def _(source=source):
            remote(
                mine.at[source], land.at[source], land_sem, source, (source, member), source
            ).wait()

    for q in range(sections):
        at = pl.ds(q * columns, columns)
        out_vd[:, at] = (land[q, 0].astype(jnp.float32) * gain[:, at]).astype(jnp.bfloat16)
        out_ou[:, at] = land[q, 1]
    for j in range(sections - 1):
        tok_copy(j, section).wait_send()
        fac_copy(j, section).wait_send()
        p_copy(j, section).wait_send()
        q_copy(j, section).wait_send()
        for layer in range(sections):
            sum_copy(fx_out, fx_in, fx_sem, layer, j).wait_send()
            sum_copy(bx_out, bx_in, bx_sem, layer, j).wait_send()
    for layer in range(sections):

        @pl.when(section != layer)
        def _(layer=layer):
            sib_weight(pbuf, psib_sem, layer).wait_send()
            sib_weight(qbuf, qsib_sem, layer).wait_send()

    line_sent(x0, x_up, x_down, x_sib)
    line_sent(cot, c_up, c_down, c_sib)


def kernel_body(
    inputs,
    cotangent,
    norm_gain,
    w_value,
    w_out,
    value_down,
    value_up_factor,
    out_down,
    output_up_factor,
    block_tenant,
    valid_tokens,
    tenant_slot,
):
    sections, members = lax.axis_size("pipe"), lax.axis_size("dp")
    member = lax.axis_index("dp")
    row_count, width = inputs.shape[1:]
    micro_count = inputs.shape[0] * sections
    columns, row_total = width // sections, micro_count * row_count * members
    rank, hd = value_up_factor.shape[2:]
    half, ranks = hd // 2, hd + rank
    gain = norm_gain[0][None]

    def folded(rows):
        return (rows.astype(jnp.float32) * gain).astype(jnp.bfloat16)

    wts = jnp.concatenate(
        [
            folded(w_value[0, :half]),
            folded(value_down[0, 0]),
            folded(w_value[0, half:]),
            w_out[0, :half],
            output_up_factor[0, 0],
            w_out[0, half:],
        ]
    )
    tok = jnp.concatenate([inputs[0], cotangent[0]])
    up, down = value_up_factor[0, 0], out_down[0, 0]
    pad = ((0, 0), (0, hd - rank))
    fac = jnp.concatenate(
        [
            jnp.concatenate([up, down], axis=1),
            jnp.concatenate([jnp.pad(up.T, pad), jnp.pad(down.T, pad)], axis=1),
        ]
    )
    weight = row_weights(
        block_tenant, valid_tokens, tenant_slot, member, micro_count, row_count
    ).reshape(-1, 1)
    half_type, levels = jnp.bfloat16, members // 2
    dma = pltpu.SemaphoreType.DMA
    vmem, anywhere = pl.BlockSpec(memory_space=pltpu.VMEM), pl.BlockSpec(memory_space=pl.ANY)
    sums = sections * (sections - 1)
    outs = pl.pallas_call(
        functools.partial(columns_kernel, (sections, members)),
        out_shape=(
            jax.ShapeDtypeStruct((rank, width), half_type),
            jax.ShapeDtypeStruct((rank, hd), half_type),
            jax.ShapeDtypeStruct((rank, hd), half_type),
            jax.ShapeDtypeStruct((rank, width), half_type),
        ),
        in_specs=[anywhere, anywhere, anywhere, vmem, vmem],
        out_specs=(vmem, vmem, vmem, vmem),
        scratch_shapes=[
            pltpu.VMEM((sections, row_total, columns), half_type),
            pltpu.VMEM((sections, row_total, columns), half_type),
            pltpu.VMEM((row_total, columns), half_type),
            pltpu.VMEM((sections, 2 * row_count, columns), half_type),
            pltpu.VMEM((sections, ranks, columns), half_type),
            pltpu.VMEM((sections, ranks, columns), half_type),
            pltpu.VMEM((sections,) + fac.shape, half_type),
            pltpu.VMEM((row_total, 128), half_type),
            pltpu.VMEM((sections, 2, rank, columns), half_type),
            pltpu.VMEM((sections, 2, rank, columns), half_type),
            pltpu.VMEM((sections, ranks + 16, row_total), half_type),
            pltpu.VMEM((sections, sections - 1, ranks + 16, row_total), half_type),
            pltpu.VMEM((sections, ranks, row_total), half_type),
            pltpu.VMEM((sections, sections - 1, ranks, row_total), half_type),
            dma((4,)),
            dma((2, sections)),
            dma((2, sections)),
            dma((2, sections)),
            dma((2, sections)),
            dma((2, sections)),
            dma((2, sections)),
            dma((2, levels)),
            dma((2, levels)),
            dma((2, levels)),
            dma((2, levels)),
            dma((2, levels)),
            dma((2, levels)),
            dma((2, sums)),
            dma((2, sums)),
            dma((2, sections)),
        ],
        compiler_params=pltpu.CompilerParams(
            collective_id=0, has_side_effects=True, vmem_limit_bytes=50 * 2**20
        ),
    )(tok, wts, fac, weight, gain)
    return tuple(part[None, None] for part in outs)


def solution(mesh):
    sections = mesh.shape["pipe"]

    def run(*arrays):
        depth, row_total, width = arrays[0].shape
        kept_bytes = 2 * depth * row_total * (width // sections) * sections
        chosen = kernel_body if kept_bytes <= stash_limit else relay_body
        return place(chosen)(*arrays)

    def place(chosen):
        return jax.shard_map(
            chosen,
            mesh=mesh,
            in_specs=(
                P("pipe", "dp", None),
                P("pipe", "dp", None),
                P("pipe", None),
                P("pipe", None, None),
                P("pipe", None, None),
                P("pipe", "dp", None, None),
                P("pipe", "dp", None, None),
                P("pipe", "dp", None, None),
                P("pipe", "dp", None, None),
                P(),
                P(),
                P(),
            ),
            out_specs=(
                P("pipe", "dp", None, None),
                P("pipe", "dp", None, None),
                P("pipe", "dp", None, None),
                P("pipe", "dp", None, None),
            ),
            check_vma=False,
        )

    return run
```

```python
import functools

import jax
import jax.numpy as jnp
from jax import lax
from jax.experimental import pallas as pl
from jax.experimental.pallas import tpu as pltpu
from jax.sharding import PartitionSpec as P

adapter_scale = 2.0
norm_eps = 1e-05
stash_limit = 8 * 2**20


def from_behind(value, axis, by):
    peers = lax.axis_size(axis)
    return lax.ppermute(value, axis, [(i, (i + by) % peers) for i in range(peers)])


def normalize(token_rows, gain_row):
    wide_rows = token_rows.astype(jnp.float32)
    inverse = lax.rsqrt(jnp.mean(wide_rows * wide_rows, axis=-1, keepdims=True) + norm_eps)
    return ((wide_rows * inverse * gain_row).astype(jnp.bfloat16), inverse)


def contract_trailing(left, right):
    return lax.dot_general(
        left, right, (((1,), (1,)), ((), ())), preferred_element_type=jnp.float32
    )


def contract_leading(left, right):
    return lax.dot_general(
        left, right, (((0,), (0,)), ((), ())), preferred_element_type=jnp.float32
    )


def section_parts(token_rows, gain_row, value_weight, tenant_adapters):
    value_down, value_up_factor, out_down, output_up_factor = tenant_adapters
    normalized_rows, inverse = normalize(token_rows, gain_row)
    lowrank_product = contract_trailing(normalized_rows, value_down).astype(jnp.bfloat16)
    value_blend = contract_trailing(normalized_rows, value_weight)
    value_blend = value_blend + adapter_scale * jnp.dot(
        lowrank_product, value_up_factor, preferred_element_type=jnp.float32
    )
    value_row_block = value_blend.astype(jnp.bfloat16)
    sidepath_rank = contract_trailing(value_row_block, out_down).astype(jnp.bfloat16)
    return (normalized_rows, inverse, lowrank_product, value_row_block, sidepath_rank)


def section_output(token_rows, layer_pieces, out_weight, tenant_adapters):
    blended_rows = token_rows.astype(jnp.float32) + jnp.dot(
        layer_pieces[3], out_weight, preferred_element_type=jnp.float32
    )
    blended_rows = blended_rows + adapter_scale * jnp.dot(
        layer_pieces[4], tenant_adapters[3], preferred_element_type=jnp.float32
    )
    return blended_rows.astype(jnp.bfloat16)


def section_backward(
    token_rows, input_gradient, layer_pieces, gain_row, value_weight, out_weight, tenant_adapters
):
    value_down, value_up_factor, out_down, output_up_factor = tenant_adapters
    normalized_rows, inverse, lowrank_product, value_row_block, sidepath_rank = layer_pieces
    sidepath_gradient = (
        adapter_scale * contract_trailing(input_gradient, output_up_factor)
    ).astype(jnp.bfloat16)
    value_gradient = contract_trailing(input_gradient, out_weight)
    value_gradient = (
        value_gradient + jnp.dot(sidepath_gradient, out_down, preferred_element_type=jnp.float32)
    ).astype(jnp.bfloat16)
    lowrank_gradient = (adapter_scale * contract_trailing(value_gradient, value_up_factor)).astype(
        jnp.bfloat16
    )
    grad_normed = jnp.dot(
        value_gradient, value_weight, preferred_element_type=jnp.float32
    ) + jnp.dot(lowrank_gradient, value_down, preferred_element_type=jnp.float32)
    scaled = grad_normed * gain_row
    wide_rows = token_rows.astype(jnp.float32)
    correction = jnp.mean(scaled * wide_rows, axis=-1, keepdims=True)
    grad_rows = inverse * scaled - wide_rows * (inverse * inverse * inverse) * correction
    grad_out = (input_gradient.astype(jnp.float32) + grad_rows).astype(jnp.bfloat16)
    gradient_pieces = (
        contract_leading(lowrank_gradient, normalized_rows),
        adapter_scale * contract_leading(lowrank_product, value_gradient),
        contract_leading(sidepath_gradient, value_row_block),
        adapter_scale * contract_leading(sidepath_rank, input_gradient),
    )
    return (grad_out, gradient_pieces)


def pass_section(token_rows, shift_by):
    return from_behind(token_rows, "pipe", shift_by)


def owner_layout(first, second, third, fourth):
    return (
        lax.all_to_all(first, "dp", split_axis=0, concat_axis=2, tiled=True),
        lax.all_to_all(second, "dp", split_axis=0, concat_axis=2, tiled=True),
        lax.all_to_all(third, "dp", split_axis=0, concat_axis=2, tiled=True),
        lax.all_to_all(fourth, "dp", split_axis=0, concat_axis=2, tiled=True),
    )


def pick_rows(picker, sliced_part):
    flat_rows = sliced_part.reshape(sliced_part.shape[0], -1)
    chosen = jnp.dot(picker, flat_rows, preferred_element_type=jnp.float32).astype(jnp.bfloat16)
    return chosen.reshape((picker.shape[0],) + sliced_part.shape[1:])


def sum_by_slot(slot_float, gathered_part):
    flat_rows = gathered_part.reshape(gathered_part.shape[0], -1)
    summed = lax.dot_general(
        slot_float,
        flat_rows,
        (((0,), (0,)), ((), ())),
        precision=lax.Precision.HIGHEST,
        preferred_element_type=jnp.float32,
    )
    return summed.astype(jnp.bfloat16).reshape((slot_float.shape[1],) + gathered_part.shape[1:])


def put_entry(stash, entry, micro_index, active):

    def update(stored_all, new_entry):
        previous = lax.dynamic_index_in_dim(stored_all, micro_index, 0, keepdims=False)
        return lax.dynamic_update_index_in_dim(
            stored_all, jnp.where(active, new_entry, previous), micro_index, 0
        )

    return jax.tree.map(update, stash, entry)


def get_entry(stash, micro_index):
    return jax.tree.map(
        lambda stored_all: lax.dynamic_index_in_dim(stored_all, micro_index, 0, keepdims=False),
        stash,
    )


def relay_body(
    inputs,
    cotangent,
    norm_gain,
    w_value,
    w_out,
    value_down,
    value_up_factor,
    out_down,
    output_up_factor,
    block_tenant,
    valid_tokens,
    tenant_slot,
):
    section_index = lax.axis_index("pipe")
    sections = lax.axis_size("pipe")
    member = lax.axis_index("dp")
    members = lax.axis_size("dp")
    queue_depth = inputs.shape[0]
    row_count = inputs.shape[1]
    micro_count = queue_depth * sections
    ticks = micro_count + sections - 1
    tenant_ids = jnp.arange(tenant_slot.shape[0], dtype=jnp.int32)
    tenant_hot = block_tenant[:, None] == tenant_ids[None, :]
    slot_of = jnp.sum(jnp.where(tenant_hot, tenant_slot[None, :], 0), axis=1)
    slot_hot = slot_of[:, None] == tenant_ids[None, :]
    member_hot = jnp.arange(members, dtype=jnp.int32) == member
    own_tenant = jnp.sum(jnp.where(member_hot, block_tenant, 0))
    own_valid = jnp.sum(jnp.where(member_hot, valid_tokens, 0))
    tenant_tokens = jnp.sum(jnp.where(block_tenant == own_tenant, valid_tokens, 0)).astype(
        jnp.float32
    )
    sliced = (
        lax.all_to_all(value_down[0], "dp", split_axis=2, concat_axis=0, tiled=True),
        lax.all_to_all(value_up_factor[0], "dp", split_axis=2, concat_axis=0, tiled=True),
        lax.all_to_all(out_down[0], "dp", split_axis=2, concat_axis=0, tiled=True),
        lax.all_to_all(output_up_factor[0], "dp", split_axis=2, concat_axis=0, tiled=True),
    )
    picker = slot_hot.astype(jnp.bfloat16)
    picked = [pick_rows(picker, sliced_part) for sliced_part in sliced]
    fetched = owner_layout(picked[0], picked[1], picked[2], picked[3])
    tenant_adapters = tuple((whole_part[0] for whole_part in fetched))
    gain_row = norm_gain[0]
    value_weight = w_value[0]
    out_weight = w_out[0]

    def token_weight(micro_index):
        position = micro_index * row_count + jnp.arange(row_count, dtype=jnp.int32)
        return (
            jnp.where(position < own_valid, 1.0, 0.0).astype(jnp.float32)[:, None] / tenant_tokens
        )

    def keep_entry(current):
        return (current,)

    def parts_of(entry):
        return section_parts(entry[0], gain_row, value_weight, tenant_adapters)

    blank = jnp.zeros((row_count, inputs.shape[2]), jnp.bfloat16)
    sample = keep_entry(blank)
    stash = jax.tree.map(
        lambda leaf_value: jnp.zeros((micro_count,) + leaf_value.shape, leaf_value.dtype), sample
    )
    accum = tuple((jnp.zeros(adapter_part.shape, jnp.float32) for adapter_part in tenant_adapters))

    def forward_tick(tick_index, arriving, feed_rows, stash_now, order):
        position = tick_index - section_index
        active = (position >= 0) & (position < micro_count)
        micro_index = order(jnp.clip(position, 0, micro_count - 1))
        current = jnp.where(section_index == 0, feed_rows, arriving)
        layer_pieces = section_parts(current, gain_row, value_weight, tenant_adapters)
        result = section_output(current, layer_pieces, out_weight, tenant_adapters)
        stash_now = put_entry(stash_now, keep_entry(current), micro_index, active)
        return (result, stash_now)

    def backward_tick(tick_index, arriving, feed_rows, stash_now, accum_now, order):
        position = tick_index - (sections - 1 - section_index)
        active = (position >= 0) & (position < micro_count)
        micro_index = order(jnp.clip(position, 0, micro_count - 1))
        entry = get_entry(stash_now, micro_index)
        seeded = (feed_rows.astype(jnp.float32) * token_weight(micro_index)).astype(jnp.bfloat16)
        input_gradient = jnp.where(section_index == sections - 1, seeded, arriving)
        grad_out, gradient_pieces = section_backward(
            entry[0],
            input_gradient,
            parts_of(entry),
            gain_row,
            value_weight,
            out_weight,
            tenant_adapters,
        )
        accum_now = tuple(
            (
                running + jnp.where(active, addend, 0.0)
                for running, addend in zip(accum_now, gradient_pieces)
            )
        )
        return (grad_out, accum_now)

    all_inputs, all_cotangents = (
        lax.all_gather(inputs, "pipe", axis=0, tiled=True),
        lax.all_gather(cotangent, "pipe", axis=0, tiled=True),
    )

    def plain_order(position):
        return position

    def forward_step(tick_index, carry):
        arriving, stash_now = carry
        feed_rows = lax.dynamic_index_in_dim(
            all_inputs, jnp.minimum(tick_index, micro_count - 1), 0, keepdims=False
        )
        result, stash_now = forward_tick(tick_index, arriving, feed_rows, stash_now, plain_order)
        return (pass_section(result, 1), stash_now)

    arriving, stash = lax.fori_loop(0, ticks, forward_step, (blank, stash))

    def backward_step(tick_index, carry):
        arriving, accum_now = carry
        feed_rows = lax.dynamic_index_in_dim(
            all_cotangents, jnp.minimum(tick_index, micro_count - 1), 0, keepdims=False
        )
        grad_out, accum_now = backward_tick(
            tick_index, arriving, feed_rows, stash, accum_now, plain_order
        )
        return (pass_section(grad_out, sections - 1), accum_now)

    arriving, accum = lax.fori_loop(0, ticks, backward_step, (blank, accum))
    spread = (
        lax.all_to_all(
            accum[0][None].astype(jnp.bfloat16), "dp", split_axis=2, concat_axis=0, tiled=True
        ).astype(jnp.float32),
        lax.all_to_all(
            accum[1][None].astype(jnp.bfloat16), "dp", split_axis=2, concat_axis=0, tiled=True
        ).astype(jnp.float32),
        lax.all_to_all(
            accum[2][None].astype(jnp.bfloat16), "dp", split_axis=2, concat_axis=0, tiled=True
        ).astype(jnp.float32),
        lax.all_to_all(
            accum[3][None].astype(jnp.bfloat16), "dp", split_axis=2, concat_axis=0, tiled=True
        ).astype(jnp.float32),
    )
    slot_float = slot_hot.astype(jnp.float32)
    totals = [sum_by_slot(slot_float, gathered_part) for gathered_part in spread]
    owned = owner_layout(totals[0], totals[1], totals[2], totals[3])
    return (owned[0][None], owned[1][None], owned[2][None], owned[3][None])


def trail(left, right):
    return lax.dot_general(
        left, right, (((1,), (1,)), ((), ())), preferred_element_type=jnp.float32
    )


def plain(left, right):
    return jnp.dot(left, right, preferred_element_type=jnp.float32)


def row_weights(block_tenant, valid_tokens, tenant_slot, member, micro_count, row_count):
    tenant_ids = jnp.arange(tenant_slot.shape[0], dtype=jnp.int32)
    tenant_hot = block_tenant[:, None] == tenant_ids[None, :]
    slot_of = jnp.sum(jnp.where(tenant_hot, tenant_slot[None, :], 0), axis=1)
    same = block_tenant[:, None] == block_tenant[None, :]
    tokens = jnp.sum(jnp.where(same, valid_tokens[None, :], 0), axis=1).astype(jnp.float32)
    position = jnp.arange(micro_count * row_count, dtype=jnp.int32)
    keep = (position[None, :] < valid_tokens[:, None]) & (slot_of[:, None] == member)
    return jnp.where(keep, 1.0, 0.0).astype(jnp.float32) / tokens[:, None]


def columns_kernel(
    shape,
    tok,
    w_into,
    a_into,
    w_outof,
    a_outof,
    gain_row,
    fac,
    row_weight,
    gain,
    out_vd,
    out_vu,
    out_od,
    out_ou,
    hid,
    grad,
    cot,
    tbuf,
    praw,
    pbuf,
    qbuf,
    fbuf,
    gbuf,
    turned,
    land,
    mine,
    fx_out,
    fx_in,
    bx_out,
    bx_in,
    local_sem,
    tok_sem,
    fac_sem,
    gain_sem,
    p_sem,
    pa_sem,
    q_sem,
    qa_sem,
    psib_sem,
    qsib_sem,
    x_up,
    x_down,
    x_sib,
    c_up,
    c_down,
    c_sib,
    fx_sem,
    bx_sem,
    land_sem,
):
    sections, members = shape
    levels = members // 2
    section, member = lax.axis_index("pipe"), lax.axis_index("dp")
    core, level = lax.rem(member, 2), lax.div(member, 2)
    sibling = (section, member + 1 - 2 * core)
    row_total, columns = hid.shape[1:]
    block = row_total // members
    width = columns * sections
    rank, hd = out_vu.shape
    half, ranks = hd // 2, hd + rank
    row_half = row_total // 2
    near = lax.div(level, levels // 2) * row_half
    half_rows = [
        pl.ds(pl.multiple_of(near, row_half), row_half),
        pl.ds(pl.multiple_of(row_half - near, row_half), row_half),
    ]
    peers = [lax.rem(section + j, sections) for j in range(1, sections)]
    step = min(512, columns)
    chunks = columns // step

    def remote(src, dst, sem, slot, target, got=None):
        return pltpu.make_async_remote_copy(
            src_ref=src,
            dst_ref=dst,
            send_sem=sem.at[0, slot],
            recv_sem=sem.at[1, slot if got is None else got],
            device_id=target,
            device_id_type=pl.DeviceIdType.MESH,
        )

    barrier = pltpu.get_barrier_semaphore()
    greeted = [(q, member) for q in peers] + [sibling]
    greeted += [(section, lax.rem(member + by, members)) for by in (2, members - 2)]
    for target in greeted:
        pl.semaphore_signal(
            barrier, inc=1, device_id=target, device_id_type=pl.DeviceIdType.MESH
        )
    own_columns = pl.ds(pl.multiple_of(section * columns, columns), columns)
    local = [
        pltpu.make_async_copy(tok.at[:, own_columns], tbuf.at[section], local_sem.at[0]),
        pltpu.make_async_copy(fac, fbuf.at[section], local_sem.at[1]),
        pltpu.make_async_copy(
            w_into.at[:, own_columns], praw.at[section, pl.ds(0, hd)], local_sem.at[2]
        ),
        pltpu.make_async_copy(
            a_into.at[:, own_columns], praw.at[section, pl.ds(hd, rank)], local_sem.at[3]
        ),
        pltpu.make_async_copy(
            w_outof.at[:, own_columns], qbuf.at[section, pl.ds(0, hd)], local_sem.at[4]
        ),
        pltpu.make_async_copy(
            a_outof.at[:, own_columns], qbuf.at[section, pl.ds(hd, rank)], local_sem.at[5]
        ),
        pltpu.make_async_copy(gain_row.at[:, own_columns], gbuf.at[section], local_sem.at[6]),
    ]
    for copy in local:
        copy.start()
    pl.semaphore_wait(barrier, len(greeted))

    share_rows = pl.ds(pl.multiple_of(core * half, half), half)
    rank_rows = pl.ds(hd, rank)

    def to_columns(q):
        return pl.ds(pl.multiple_of(q * columns, columns), columns)

    def tok_copy(j, src_section):
        q = peers[j]
        return remote(
            tok.at[:, to_columns(q)], tbuf.at[src_section], tok_sem, j, (q, member), src_section
        )

    def fac_copy(j, src_section):
        return remote(fac, fbuf.at[src_section], fac_sem, j, (peers[j], member), src_section)

    def gain_copy(j, src_section):
        q = peers[j]
        return remote(
            gain_row.at[:, to_columns(q)],
            gbuf.at[src_section],
            gain_sem,
            j,
            (q, member),
            src_section,
        )

    def weight_copy(src, buf, sem):
        def copy_of(j, src_section):
            q = peers[j]
            return remote(
                src.at[share_rows, to_columns(q)],
                buf.at[src_section, share_rows],
                sem,
                j,
                (q, member),
                src_section,
            )

        return copy_of

    def adapter_copy(src, buf, sem):
        def copy_of(j, src_section):
            q = peers[j]
            return remote(
                src.at[:, to_columns(q)],
                buf.at[src_section, rank_rows],
                sem,
                j,
                (q, member),
                src_section,
            )

        return copy_of

    p_copy, pa_copy = weight_copy(w_into, praw, p_sem), adapter_copy(a_into, praw, pa_sem)
    q_copy, qa_copy = weight_copy(w_outof, qbuf, q_sem), adapter_copy(a_outof, qbuf, qa_sem)

    def sib_weight(buf, sem, layer):
        piece = buf.at[layer, share_rows]
        return remote(piece, piece, sem, layer, sibling)

    def arrive(copy_of, layer):
        @pl.when(section != layer)
        def _():
            copy_of(0, layer).wait_recv()

    def arrive_and_pass(copy_of, buf, sem, layer):
        @pl.when(section != layer)
        def _():
            copy_of(0, layer).wait_recv()
            sib_weight(buf, sem, layer).start()

    def passed(buf, sem, layer):
        @pl.when(section != layer)
        def _():
            sib_weight(buf, sem, layer).wait_recv()

    def block_rows(buf, at_level):
        start = pl.multiple_of((at_level * 2 + core) * block, block)
        return buf.at[pl.ds(start, block)]

    def up_copy(buf, sem, k):
        piece = block_rows(buf, level - k)
        return remote(piece, piece, sem, k, (section, member + 2))

    def down_copy(buf, sem, k):
        piece = block_rows(buf, level + k)
        return remote(piece, piece, sem, k, (section, member - 2))

    def sib_copy(buf, sem, at_level):
        piece = block_rows(buf, at_level)
        return remote(piece, piece, sem, at_level, sibling)

    def line_start(buf, up, down, k):
        @pl.when((level < levels - 1) & (level - k >= 0))
        def _():
            up_copy(buf, up, k).start()

        @pl.when((level > 0) & (level + k < levels))
        def _():
            down_copy(buf, down, k).start()

    def line_arrive(buf, up, down, sib, k):
        @pl.when(level - 1 - k >= 0)
        def _():
            up_copy(buf, up, k).wait_recv()

        @pl.when(level + 1 + k < levels)
        def _():
            down_copy(buf, down, k).wait_recv()

        if k + 1 < levels - 1:
            line_start(buf, up, down, k + 1)

        @pl.when(level - 1 - k >= 0)
        def _():
            sib_copy(buf, sib, level - 1 - k).start()

        @pl.when(level + 1 + k < levels)
        def _():
            sib_copy(buf, sib, level + 1 + k).start()

    def line_sent(buf, up, down, sib):
        for k in range(levels - 1):

            @pl.when((level < levels - 1) & (level - k >= 0))
            def _(k=k):
                up_copy(buf, up, k).wait_send()

            @pl.when((level > 0) & (level + k < levels))
            def _(k=k):
                down_copy(buf, down, k).wait_send()

        for at_level in range(levels):
            sib_copy(buf, sib, at_level).wait_send()

    def sum_copy(out, into, sem, layer, part, j):
        return remote(
            out.at[layer, part],
            into.at[layer, part, j],
            sem,
            (layer * 2 + part) * (sections - 1) + j,
            (peers[j], member),
        )

    def send_sum(out, into, sem, layer, part, partial):
        out[layer, part] = partial.astype(jnp.bfloat16)
        for j in range(sections - 1):
            sum_copy(out, into, sem, layer, part, j).start()

    def whole_sum(out, into, sem, layer, part, partial):
        for j in range(sections - 1):
            sum_copy(out, into, sem, layer, part, j).wait_recv()
        for j in range(sections - 1):
            partial = partial + into[layer, part, j].astype(jnp.float32)
        return partial

    for j in range(sections - 1):
        tok_copy(j, section).start()
    for j in range(sections - 1):
        p_copy(j, section).start()
        pa_copy(j, section).start()
        gain_copy(j, section).start()
        fac_copy(j, section).start()

    local[0].wait()
    for layer in range(sections):
        arrive(tok_copy, layer)
    per = block // sections
    for t in range(chunks):
        at = pl.ds(t * step, step)
        wide = [tbuf[m, :, at].astype(jnp.float32) for m in range(sections)]
        own = pl.ds(pl.multiple_of(member * block, block), block)
        hid[0, own, at] = jnp.concatenate([w[:per] for w in wide]).astype(jnp.bfloat16)
        cot[own, at] = jnp.concatenate([w[per:] for w in wide]).astype(jnp.bfloat16)
    x0 = hid.at[0]
    line_start(x0, x_up, x_down, 0)
    sib_copy(x0, x_sib, level).start()
    for j in range(sections - 1):
        q_copy(j, section).start()
        qa_copy(j, section).start()
    for copy in local[1:]:
        copy.wait()

    ones = jnp.ones((16, 128), jnp.bfloat16)

    def chunk(t):
        return pl.ds(pl.multiple_of(t * step, step), step)

    def project(layer, at, wide, rows):
        squares = wide * wide
        lanes = squares[:, :128]
        for start in range(128, step, 128):
            lanes = lanes + squares[:, start : start + 128]
        return trail(pbuf[layer, :, at], rows), lanes

    def add(left, right):
        return tuple(a + b for a, b in zip(left, right))

    zero_back = jnp.zeros((ranks, row_half), jnp.float32)
    zero_sum = (zero_back, jnp.zeros((row_half, 128), jnp.float32))

    def send_forward(layer, part, total):
        lanes = total[1]
        high = lanes.astype(jnp.bfloat16)
        low = (lanes - high.astype(jnp.float32)).astype(jnp.bfloat16)
        squares = (trail(ones, high) + trail(ones, low))[:8]
        high = squares.astype(jnp.bfloat16).astype(jnp.float32)
        partial = jnp.concatenate([total[0], high, squares - high])
        send_sum(fx_out, fx_in, fx_sem, layer, part, partial)
        return partial

    def turn(parts):
        parts = jnp.concatenate(parts)
        spare = jnp.zeros((128 - parts.shape[0], row_half), jnp.float32)
        return jnp.concatenate([parts, spare]).T

    def in_order(parts):
        wide = [part.astype(jnp.float32) for part in parts]
        straight, swapped = jnp.concatenate(wide, axis=1), jnp.concatenate(wide[::-1], axis=1)
        return jnp.where(near == 0, straight, swapped).astype(jnp.bfloat16)

    def fold(layer):
        passed(praw, psib_sem, layer)
        pbuf[layer] = (praw[layer].astype(jnp.float32) * gbuf[layer]).astype(jnp.bfloat16)

    def take_first(part):
        def first(t, total):
            rows = hid[0, half_rows[part], chunk(t)]
            return add(total, project(0, chunk(t), rows.astype(jnp.float32), rows))

        return send_forward(0, part, lax.fori_loop(0, chunks, first, zero_sum, unroll=True))

    def line_levels(buf, sib, wanted):
        for at_level in range(levels):

            @pl.when((lax.div(at_level, levels // 2) == lax.div(level, levels // 2)) == wanted)
            def _(at_level=at_level):
                sib_copy(buf, sib, at_level).wait_recv()

    reach = levels // 2 - 1
    for k in range(reach):
        line_arrive(x0, x_up, x_down, x_sib, k)
    for layer in range(sections):
        arrive_and_pass(p_copy, praw, psib_sem, layer)
        arrive(pa_copy, layer)
        arrive(gain_copy, layer)
        arrive(fac_copy, layer)
    fold(0)
    line_levels(x0, x_sib, True)
    partials = [take_first(0)]
    for k in range(reach, levels - 1):
        line_arrive(x0, x_up, x_down, x_sib, k)
    line_start(cot, c_up, c_down, 0)
    sib_copy(cot, c_sib, level).start()
    line_levels(x0, x_sib, False)
    partials.append(take_first(1))

    last = sections - 1
    kept, sides, backs = [], [], [None, None]
    for layer in range(sections):
        if layer < last:
            fold(layer + 1)
        if layer == 0:
            arrive_and_pass(q_copy, qbuf, qsib_sem, 0)
            arrive(qa_copy, 0)
        if layer == 1:
            for later in range(1, sections):
                arrive_and_pass(q_copy, qbuf, qsib_sem, later)
                arrive(qa_copy, later)
        if layer < levels - 1:
            line_arrive(cot, c_up, c_down, c_sib, layer)
        passed(qbuf, qsib_sem, layer)
        if layer == last:
            for k in range(last + 1, levels - 1):
                line_arrive(cot, c_up, c_down, c_sib, k)
            for at_level in range(levels):
                sib_copy(cot, c_sib, at_level).wait_recv()
            for part in range(2):
                rows_of = half_rows[part]

                def seed(t, total_now, rows_of=rows_of):
                    at = chunk(t)
                    top = cot[rows_of, at].astype(jnp.float32) * row_weight[rows_of, :]
                    top = top.astype(jnp.bfloat16)
                    grad[last, rows_of, at] = top
                    return total_now + trail(qbuf[last, :, at], top)

                backs[part] = lax.fori_loop(0, chunks, seed, zero_back, unroll=True)
                send_sum(bx_out, bx_in, bx_sem, last, part, backs[part])
        factor = fbuf[layer]
        halves = []
        for part in range(2):
            rows_of = half_rows[part]
            whole = whole_sum(fx_out, fx_in, fx_sem, layer, part, partials[part])
            projection = whole[:ranks]
            squares = whole[ranks : ranks + 1] + whole[ranks + 8 : ranks + 9]
            inverse = lax.rsqrt(squares / width + norm_eps)
            scaled = projection * inverse
            lowrank = scaled[hd:].astype(jnp.bfloat16)
            value = (
                scaled[:hd] + adapter_scale * plain(factor[rank:, :rank], lowrank)
            ).astype(jnp.bfloat16)
            side = plain(factor[:rank, hd : 2 * hd], value).astype(jnp.bfloat16)
            halves.append((projection, inverse, lowrank, value, side))
            if layer < last:
                mixed = [value.astype(jnp.float32), adapter_scale * side.astype(jnp.float32)]
                turned[part] = turn(mixed).astype(jnp.bfloat16)

                def update(t, total_now, layer=layer, part=part, rows_of=rows_of):
                    at = chunk(t)
                    rows = hid[layer, rows_of, at].astype(jnp.float32)
                    rows = rows + plain(turned[part, :, :ranks], qbuf[layer, :, at])
                    rows = rows.astype(jnp.bfloat16)
                    hid[layer + 1, rows_of, at] = rows
                    return add(
                        total_now, project(layer + 1, at, rows.astype(jnp.float32), rows)
                    )

                total = lax.fori_loop(0, chunks, update, zero_sum, unroll=True)
                partials[part] = send_forward(layer + 1, part, total)
        kept.append(halves)
        sides.append(in_order([h[4] for h in halves]))

    def land_copy(layer, which):
        return remote(
            mine.at[layer, which],
            land.at[section, which],
            land_sem,
            layer * 2 + which,
            (layer, member),
            section * 2 + which,
        )

    def collect(layer, which, small, wide, by):
        def gather(t, carry):
            at = chunk(t)
            mine[layer, which, :, at] = (by * plain(small, wide[layer, :, at])).astype(
                jnp.bfloat16
            )
            return carry

        lax.fori_loop(0, chunks, gather, 0, unroll=True)

        @pl.when(section != layer)
        def _():
            land_copy(layer, which).start()

        @pl.when(section == layer)
        def _():
            land[layer, which] = mine[layer, which]

    collect(last, 1, sides[last], grad, adapter_scale)
    for layer in reversed(range(sections)):
        factor = fbuf[layer]
        lows, small_up, small_down = [], None, None
        for part in range(2):
            rows_of = half_rows[part]
            projection, inverse, lowrank, value, side = kept[layer][part]
            whole = whole_sum(bx_out, bx_in, bx_sem, layer, part, backs[part])
            grad_side = (adapter_scale * whole[hd:]).astype(jnp.bfloat16)
            grad_value = (whole[:hd] + plain(factor[rank:, hd : hd + rank], grad_side)).astype(
                jnp.bfloat16
            )
            grad_low = (adapter_scale * plain(factor[:rank, :hd], grad_value)).astype(
                jnp.bfloat16
            )
            both = jnp.concatenate(
                [grad_value.astype(jnp.float32), grad_low.astype(jnp.float32)]
            )
            scaled = both * inverse
            lows.append(scaled[hd:])
            if layer > 0:
                correction = jnp.sum(both * projection, axis=0, keepdims=True) / width
                shrink = inverse * inverse * inverse * correction
                shrink = jnp.broadcast_to(shrink, (8, row_half))
                columns_of = turn([scaled, shrink])
                turned[part] = columns_of.astype(jnp.bfloat16)
                shrink_column = columns_of[:, ranks : ranks + 1]

                def step_back(
                    t, total_now, layer=layer, part=part, rows_of=rows_of, shrink=shrink_column
                ):
                    at = chunk(t)
                    rows = hid[layer, rows_of, at].astype(jnp.float32)
                    fresh = grad[layer, rows_of, at].astype(jnp.float32)
                    fresh = fresh + plain(turned[part, :, :ranks], pbuf[layer, :, at])
                    fresh = (fresh - rows * shrink).astype(jnp.bfloat16)
                    grad[layer - 1, rows_of, at] = fresh
                    return total_now + trail(qbuf[layer - 1, :, at], fresh)

                backs[part] = lax.fori_loop(0, chunks, step_back, zero_back, unroll=True)
                send_sum(bx_out, bx_in, bx_sem, layer - 1, part, backs[part])
            up_now = trail(lowrank, grad_value)
            down_now = trail(grad_side, value)
            small_up = up_now if small_up is None else small_up + up_now
            small_down = down_now if small_down is None else small_down + down_now
        collect(layer, 0, in_order(lows), hid, 1.0)
        if layer > 0:
            collect(layer - 1, 1, sides[layer - 1], grad, adapter_scale)

        @pl.when(section == layer)
        def _(small_up=small_up, small_down=small_down):
            out_vu[...] = (adapter_scale * small_up).astype(jnp.bfloat16)
            out_od[...] = small_down.astype(jnp.bfloat16)

    def landed(source, which):
        @pl.when(section != source)
        def _():
            remote(
                mine.at[source, which],
                land.at[source, which],
                land_sem,
                source * 2 + which,
                (source, member),
                source * 2 + which,
            ).wait()

    for q in range(sections):
        landed(q, 1)
        at = pl.ds(q * columns, columns)
        out_ou[:, at] = land[q, 1]
    for j in range(sections - 1):
        for copy_of in (tok_copy, fac_copy, gain_copy, p_copy, pa_copy, q_copy, qa_copy):
            copy_of(j, section).wait_send()
        for layer in range(sections):
            for part in range(2):
                sum_copy(fx_out, fx_in, fx_sem, layer, part, j).wait_send()
                sum_copy(bx_out, bx_in, bx_sem, layer, part, j).wait_send()
    for layer in range(sections):

        @pl.when(section != layer)
        def _(layer=layer):
            sib_weight(praw, psib_sem, layer).wait_send()
            sib_weight(qbuf, qsib_sem, layer).wait_send()

    line_sent(x0, x_up, x_down, x_sib)
    line_sent(cot, c_up, c_down, c_sib)
    for q in range(sections):
        landed(q, 0)
        at = pl.ds(q * columns, columns)
        out_vd[:, at] = (land[q, 0].astype(jnp.float32) * gain[:, at]).astype(jnp.bfloat16)


def kernel_body(
    inputs,
    cotangent,
    norm_gain,
    w_value,
    w_out,
    value_down,
    value_up_factor,
    out_down,
    output_up_factor,
    block_tenant,
    valid_tokens,
    tenant_slot,
):
    sections, members = lax.axis_size("pipe"), lax.axis_size("dp")
    member = lax.axis_index("dp")
    row_count, width = inputs.shape[1:]
    micro_count = inputs.shape[0] * sections
    columns, row_total = width // sections, micro_count * row_count * members
    rank, hd = value_up_factor.shape[2:]
    ranks, row_half = hd + rank, row_total // 2
    tok = jnp.concatenate([inputs[0], cotangent[0]])
    up, down = value_up_factor[0, 0], out_down[0, 0]
    pad = ((0, 0), (0, hd - rank))
    fac = jnp.concatenate(
        [
            jnp.concatenate([up, down], axis=1),
            jnp.concatenate([jnp.pad(up.T, pad), jnp.pad(down.T, pad)], axis=1),
        ]
    )
    weight = row_weights(
        block_tenant, valid_tokens, tenant_slot, member, micro_count, row_count
    ).reshape(-1, 1)
    half_type, levels = jnp.bfloat16, members // 2
    dma = pltpu.SemaphoreType.DMA
    vmem, anywhere = pl.BlockSpec(memory_space=pltpu.VMEM), pl.BlockSpec(memory_space=pl.ANY)
    sums = sections * (sections - 1)
    outs = pl.pallas_call(
        functools.partial(columns_kernel, (sections, members)),
        out_shape=(
            jax.ShapeDtypeStruct((rank, width), half_type),
            jax.ShapeDtypeStruct((rank, hd), half_type),
            jax.ShapeDtypeStruct((rank, hd), half_type),
            jax.ShapeDtypeStruct((rank, width), half_type),
        ),
        in_specs=[anywhere] * 7 + [vmem, vmem],
        out_specs=(vmem, vmem, vmem, vmem),
        scratch_shapes=[
            pltpu.VMEM((sections, row_total, columns), half_type),
            pltpu.VMEM((sections, row_total, columns), half_type),
            pltpu.VMEM((row_total, columns), half_type),
            pltpu.VMEM((sections, 2 * row_count, columns), half_type),
            pltpu.VMEM((sections, ranks, columns), half_type),
            pltpu.VMEM((sections, ranks, columns), half_type),
            pltpu.VMEM((sections, ranks, columns), half_type),
            pltpu.VMEM((sections,) + fac.shape, half_type),
            pltpu.VMEM((sections, 1, columns), jnp.float32),
            pltpu.VMEM((2, row_half, 128), half_type),
            pltpu.VMEM((sections, 2, rank, columns), half_type),
            pltpu.VMEM((sections, 2, rank, columns), half_type),
            pltpu.VMEM((sections, 2, ranks + 16, row_half), half_type),
            pltpu.VMEM((sections, 2, sections - 1, ranks + 16, row_half), half_type),
            pltpu.VMEM((sections, 2, ranks, row_half), half_type),
            pltpu.VMEM((sections, 2, sections - 1, ranks, row_half), half_type),
            dma((7,)),
            dma((2, sections)),
            dma((2, sections)),
            dma((2, sections)),
            dma((2, sections)),
            dma((2, sections)),
            dma((2, sections)),
            dma((2, sections)),
            dma((2, sections)),
            dma((2, sections)),
            dma((2, levels)),
            dma((2, levels)),
            dma((2, levels)),
            dma((2, levels)),
            dma((2, levels)),
            dma((2, levels)),
            dma((2, 2 * sums)),
            dma((2, 2 * sums)),
            dma((2, 2 * sections)),
        ],
        compiler_params=pltpu.CompilerParams(
            collective_id=0, has_side_effects=True, vmem_limit_bytes=50 * 2**20
        ),
    )(
        tok,
        w_value[0],
        value_down[0, 0],
        w_out[0],
        output_up_factor[0, 0],
        norm_gain,
        fac,
        weight,
        norm_gain,
    )
    return tuple(part[None, None] for part in outs)


def solution(mesh):
    sections = mesh.shape["pipe"]

    def run(*arrays):
        depth, row_total, width = arrays[0].shape
        kept_bytes = 2 * depth * row_total * (width // sections) * sections
        chosen = kernel_body if kept_bytes <= stash_limit else relay_body
        return place(chosen)(*arrays)

    def place(chosen):
        return jax.shard_map(
            chosen,
            mesh=mesh,
            in_specs=(
                P("pipe", "dp", None),
                P("pipe", "dp", None),
                P("pipe", None),
                P("pipe", None, None),
                P("pipe", None, None),
                P("pipe", "dp", None, None),
                P("pipe", "dp", None, None),
                P("pipe", "dp", None, None),
                P("pipe", "dp", None, None),
                P(),
                P(),
                P(),
            ),
            out_specs=(
                P("pipe", "dp", None, None),
                P("pipe", "dp", None, None),
                P("pipe", "dp", None, None),
                P("pipe", "dp", None, None),
            ),
            check_vma=False,
        )

    return run
```

```python
import functools

import jax
import jax.numpy as jnp
from jax import lax
from jax.experimental import pallas as pl
from jax.experimental.pallas import tpu as pltpu
from jax.sharding import PartitionSpec as P

adapter_scale = 2.0
norm_eps = 1e-05
stash_limit = 8 * 2**20


def from_behind(value, axis, by):
    peers = lax.axis_size(axis)
    return lax.ppermute(value, axis, [(i, (i + by) % peers) for i in range(peers)])


def normalize(token_rows, gain_row):
    wide_rows = token_rows.astype(jnp.float32)
    inverse = lax.rsqrt(jnp.mean(wide_rows * wide_rows, axis=-1, keepdims=True) + norm_eps)
    return ((wide_rows * inverse * gain_row).astype(jnp.bfloat16), inverse)


def contract_trailing(left, right):
    return lax.dot_general(
        left, right, (((1,), (1,)), ((), ())), preferred_element_type=jnp.float32
    )


def contract_leading(left, right):
    return lax.dot_general(
        left, right, (((0,), (0,)), ((), ())), preferred_element_type=jnp.float32
    )


def section_parts(token_rows, gain_row, value_weight, tenant_adapters):
    value_down, value_up_factor, out_down, output_up_factor = tenant_adapters
    normalized_rows, inverse = normalize(token_rows, gain_row)
    lowrank_product = contract_trailing(normalized_rows, value_down).astype(jnp.bfloat16)
    value_blend = contract_trailing(normalized_rows, value_weight)
    value_blend = value_blend + adapter_scale * jnp.dot(
        lowrank_product, value_up_factor, preferred_element_type=jnp.float32
    )
    value_row_block = value_blend.astype(jnp.bfloat16)
    sidepath_rank = contract_trailing(value_row_block, out_down).astype(jnp.bfloat16)
    return (normalized_rows, inverse, lowrank_product, value_row_block, sidepath_rank)


def section_output(token_rows, layer_pieces, out_weight, tenant_adapters):
    blended_rows = token_rows.astype(jnp.float32) + jnp.dot(
        layer_pieces[3], out_weight, preferred_element_type=jnp.float32
    )
    blended_rows = blended_rows + adapter_scale * jnp.dot(
        layer_pieces[4], tenant_adapters[3], preferred_element_type=jnp.float32
    )
    return blended_rows.astype(jnp.bfloat16)


def section_backward(
    token_rows, input_gradient, layer_pieces, gain_row, value_weight, out_weight, tenant_adapters
):
    value_down, value_up_factor, out_down, output_up_factor = tenant_adapters
    normalized_rows, inverse, lowrank_product, value_row_block, sidepath_rank = layer_pieces
    sidepath_gradient = (
        adapter_scale * contract_trailing(input_gradient, output_up_factor)
    ).astype(jnp.bfloat16)
    value_gradient = contract_trailing(input_gradient, out_weight)
    value_gradient = (
        value_gradient + jnp.dot(sidepath_gradient, out_down, preferred_element_type=jnp.float32)
    ).astype(jnp.bfloat16)
    lowrank_gradient = (adapter_scale * contract_trailing(value_gradient, value_up_factor)).astype(
        jnp.bfloat16
    )
    grad_normed = jnp.dot(
        value_gradient, value_weight, preferred_element_type=jnp.float32
    ) + jnp.dot(lowrank_gradient, value_down, preferred_element_type=jnp.float32)
    scaled = grad_normed * gain_row
    wide_rows = token_rows.astype(jnp.float32)
    correction = jnp.mean(scaled * wide_rows, axis=-1, keepdims=True)
    grad_rows = inverse * scaled - wide_rows * (inverse * inverse * inverse) * correction
    grad_out = (input_gradient.astype(jnp.float32) + grad_rows).astype(jnp.bfloat16)
    gradient_pieces = (
        contract_leading(lowrank_gradient, normalized_rows),
        adapter_scale * contract_leading(lowrank_product, value_gradient),
        contract_leading(sidepath_gradient, value_row_block),
        adapter_scale * contract_leading(sidepath_rank, input_gradient),
    )
    return (grad_out, gradient_pieces)


def pass_section(token_rows, shift_by):
    return from_behind(token_rows, "pipe", shift_by)


def owner_layout(first, second, third, fourth):
    return (
        lax.all_to_all(first, "dp", split_axis=0, concat_axis=2, tiled=True),
        lax.all_to_all(second, "dp", split_axis=0, concat_axis=2, tiled=True),
        lax.all_to_all(third, "dp", split_axis=0, concat_axis=2, tiled=True),
        lax.all_to_all(fourth, "dp", split_axis=0, concat_axis=2, tiled=True),
    )


def pick_rows(picker, sliced_part):
    flat_rows = sliced_part.reshape(sliced_part.shape[0], -1)
    chosen = jnp.dot(picker, flat_rows, preferred_element_type=jnp.float32).astype(jnp.bfloat16)
    return chosen.reshape((picker.shape[0],) + sliced_part.shape[1:])


def sum_by_slot(slot_float, gathered_part):
    flat_rows = gathered_part.reshape(gathered_part.shape[0], -1)
    summed = lax.dot_general(
        slot_float,
        flat_rows,
        (((0,), (0,)), ((), ())),
        precision=lax.Precision.HIGHEST,
        preferred_element_type=jnp.float32,
    )
    return summed.astype(jnp.bfloat16).reshape((slot_float.shape[1],) + gathered_part.shape[1:])


def put_entry(stash, entry, micro_index, active):

    def update(stored_all, new_entry):
        previous = lax.dynamic_index_in_dim(stored_all, micro_index, 0, keepdims=False)
        return lax.dynamic_update_index_in_dim(
            stored_all, jnp.where(active, new_entry, previous), micro_index, 0
        )

    return jax.tree.map(update, stash, entry)


def get_entry(stash, micro_index):
    return jax.tree.map(
        lambda stored_all: lax.dynamic_index_in_dim(stored_all, micro_index, 0, keepdims=False),
        stash,
    )


def relay_body(
    inputs,
    cotangent,
    norm_gain,
    w_value,
    w_out,
    value_down,
    value_up_factor,
    out_down,
    output_up_factor,
    block_tenant,
    valid_tokens,
    tenant_slot,
):
    section_index = lax.axis_index("pipe")
    sections = lax.axis_size("pipe")
    member = lax.axis_index("dp")
    members = lax.axis_size("dp")
    queue_depth = inputs.shape[0]
    row_count = inputs.shape[1]
    micro_count = queue_depth * sections
    ticks = micro_count + sections - 1
    tenant_ids = jnp.arange(tenant_slot.shape[0], dtype=jnp.int32)
    tenant_hot = block_tenant[:, None] == tenant_ids[None, :]
    slot_of = jnp.sum(jnp.where(tenant_hot, tenant_slot[None, :], 0), axis=1)
    slot_hot = slot_of[:, None] == tenant_ids[None, :]
    member_hot = jnp.arange(members, dtype=jnp.int32) == member
    own_tenant = jnp.sum(jnp.where(member_hot, block_tenant, 0))
    own_valid = jnp.sum(jnp.where(member_hot, valid_tokens, 0))
    tenant_tokens = jnp.sum(jnp.where(block_tenant == own_tenant, valid_tokens, 0)).astype(
        jnp.float32
    )
    sliced = (
        lax.all_to_all(value_down[0], "dp", split_axis=2, concat_axis=0, tiled=True),
        lax.all_to_all(value_up_factor[0], "dp", split_axis=2, concat_axis=0, tiled=True),
        lax.all_to_all(out_down[0], "dp", split_axis=2, concat_axis=0, tiled=True),
        lax.all_to_all(output_up_factor[0], "dp", split_axis=2, concat_axis=0, tiled=True),
    )
    picker = slot_hot.astype(jnp.bfloat16)
    picked = [pick_rows(picker, sliced_part) for sliced_part in sliced]
    fetched = owner_layout(picked[0], picked[1], picked[2], picked[3])
    tenant_adapters = tuple((whole_part[0] for whole_part in fetched))
    gain_row = norm_gain[0]
    value_weight = w_value[0]
    out_weight = w_out[0]

    def token_weight(micro_index):
        position = micro_index * row_count + jnp.arange(row_count, dtype=jnp.int32)
        return (
            jnp.where(position < own_valid, 1.0, 0.0).astype(jnp.float32)[:, None] / tenant_tokens
        )

    def keep_entry(current):
        return (current,)

    def parts_of(entry):
        return section_parts(entry[0], gain_row, value_weight, tenant_adapters)

    blank = jnp.zeros((row_count, inputs.shape[2]), jnp.bfloat16)
    sample = keep_entry(blank)
    stash = jax.tree.map(
        lambda leaf_value: jnp.zeros((micro_count,) + leaf_value.shape, leaf_value.dtype), sample
    )
    accum = tuple((jnp.zeros(adapter_part.shape, jnp.float32) for adapter_part in tenant_adapters))

    def forward_tick(tick_index, arriving, feed_rows, stash_now, order):
        position = tick_index - section_index
        active = (position >= 0) & (position < micro_count)
        micro_index = order(jnp.clip(position, 0, micro_count - 1))
        current = jnp.where(section_index == 0, feed_rows, arriving)
        layer_pieces = section_parts(current, gain_row, value_weight, tenant_adapters)
        result = section_output(current, layer_pieces, out_weight, tenant_adapters)
        stash_now = put_entry(stash_now, keep_entry(current), micro_index, active)
        return (result, stash_now)

    def backward_tick(tick_index, arriving, feed_rows, stash_now, accum_now, order):
        position = tick_index - (sections - 1 - section_index)
        active = (position >= 0) & (position < micro_count)
        micro_index = order(jnp.clip(position, 0, micro_count - 1))
        entry = get_entry(stash_now, micro_index)
        seeded = (feed_rows.astype(jnp.float32) * token_weight(micro_index)).astype(jnp.bfloat16)
        input_gradient = jnp.where(section_index == sections - 1, seeded, arriving)
        grad_out, gradient_pieces = section_backward(
            entry[0],
            input_gradient,
            parts_of(entry),
            gain_row,
            value_weight,
            out_weight,
            tenant_adapters,
        )
        accum_now = tuple(
            (
                running + jnp.where(active, addend, 0.0)
                for running, addend in zip(accum_now, gradient_pieces)
            )
        )
        return (grad_out, accum_now)

    all_inputs, all_cotangents = (
        lax.all_gather(inputs, "pipe", axis=0, tiled=True),
        lax.all_gather(cotangent, "pipe", axis=0, tiled=True),
    )

    def plain_order(position):
        return position

    def forward_step(tick_index, carry):
        arriving, stash_now = carry
        feed_rows = lax.dynamic_index_in_dim(
            all_inputs, jnp.minimum(tick_index, micro_count - 1), 0, keepdims=False
        )
        result, stash_now = forward_tick(tick_index, arriving, feed_rows, stash_now, plain_order)
        return (pass_section(result, 1), stash_now)

    arriving, stash = lax.fori_loop(0, ticks, forward_step, (blank, stash))

    def backward_step(tick_index, carry):
        arriving, accum_now = carry
        feed_rows = lax.dynamic_index_in_dim(
            all_cotangents, jnp.minimum(tick_index, micro_count - 1), 0, keepdims=False
        )
        grad_out, accum_now = backward_tick(
            tick_index, arriving, feed_rows, stash, accum_now, plain_order
        )
        return (pass_section(grad_out, sections - 1), accum_now)

    arriving, accum = lax.fori_loop(0, ticks, backward_step, (blank, accum))
    spread = (
        lax.all_to_all(
            accum[0][None].astype(jnp.bfloat16), "dp", split_axis=2, concat_axis=0, tiled=True
        ).astype(jnp.float32),
        lax.all_to_all(
            accum[1][None].astype(jnp.bfloat16), "dp", split_axis=2, concat_axis=0, tiled=True
        ).astype(jnp.float32),
        lax.all_to_all(
            accum[2][None].astype(jnp.bfloat16), "dp", split_axis=2, concat_axis=0, tiled=True
        ).astype(jnp.float32),
        lax.all_to_all(
            accum[3][None].astype(jnp.bfloat16), "dp", split_axis=2, concat_axis=0, tiled=True
        ).astype(jnp.float32),
    )
    slot_float = slot_hot.astype(jnp.float32)
    totals = [sum_by_slot(slot_float, gathered_part) for gathered_part in spread]
    owned = owner_layout(totals[0], totals[1], totals[2], totals[3])
    return (owned[0][None], owned[1][None], owned[2][None], owned[3][None])


def trail(left, right):
    return lax.dot_general(
        left, right, (((1,), (1,)), ((), ())), preferred_element_type=jnp.float32
    )


def plain(left, right):
    return jnp.dot(left, right, preferred_element_type=jnp.float32)


def row_weights(block_tenant, valid_tokens, tenant_slot, member, micro_count, row_count):
    tenant_ids = jnp.arange(tenant_slot.shape[0], dtype=jnp.int32)
    tenant_hot = block_tenant[:, None] == tenant_ids[None, :]
    slot_of = jnp.sum(jnp.where(tenant_hot, tenant_slot[None, :], 0), axis=1)
    same = block_tenant[:, None] == block_tenant[None, :]
    tokens = jnp.sum(jnp.where(same, valid_tokens[None, :], 0), axis=1).astype(jnp.float32)
    position = jnp.arange(micro_count * row_count, dtype=jnp.int32)
    keep = (position[None, :] < valid_tokens[:, None]) & (slot_of[:, None] == member)
    return jnp.where(keep, 1.0, 0.0).astype(jnp.float32) / tokens[:, None]


def columns_kernel(
    shape,
    tok,
    w_into,
    a_into,
    w_outof,
    a_outof,
    gain_row,
    fac,
    row_weight,
    gain,
    out_vd,
    out_vu,
    out_od,
    out_ou,
    hid,
    grad,
    cot,
    tbuf,
    praw,
    pbuf,
    qbuf,
    pfold,
    qfold,
    fbuf,
    gbuf,
    turned,
    land,
    mine,
    fx_out,
    fx_in,
    bx_out,
    bx_in,
    local_sem,
    tok_sem,
    fac_sem,
    gain_sem,
    p_sem,
    pa_sem,
    q_sem,
    qa_sem,
    psib_sem,
    qsib_sem,
    x_up,
    x_down,
    x_sib,
    c_up,
    c_down,
    c_sib,
    fx_sem,
    bx_sem,
    land_sem,
):
    sections, members = shape
    levels = members // 2
    section, member = lax.axis_index("pipe"), lax.axis_index("dp")
    core, level = lax.rem(member, 2), lax.div(member, 2)
    sibling = (section, member + 1 - 2 * core)
    row_total, columns = hid.shape[1:]
    block = row_total // members
    width = columns * sections
    rank, hd = out_vu.shape
    half, ranks = hd // 2, hd + rank
    row_half = row_total // 2
    near = lax.div(level, levels // 2) * row_half
    half_rows = [
        pl.ds(pl.multiple_of(near, row_half), row_half),
        pl.ds(pl.multiple_of(row_half - near, row_half), row_half),
    ]
    peers = [lax.rem(section + j, sections) for j in range(1, sections)]
    step = min(512, columns)
    chunks = columns // step

    def remote(src, dst, sem, slot, target, got=None):
        return pltpu.make_async_remote_copy(
            src_ref=src,
            dst_ref=dst,
            send_sem=sem.at[0, slot],
            recv_sem=sem.at[1, slot if got is None else got],
            device_id=target,
            device_id_type=pl.DeviceIdType.MESH,
        )

    barrier = pltpu.get_barrier_semaphore()
    greeted = [(q, member) for q in peers] + [sibling]
    greeted += [(section, lax.rem(member + by, members)) for by in (2, members - 2)]
    for target in greeted:
        pl.semaphore_signal(
            barrier, inc=1, device_id=target, device_id_type=pl.DeviceIdType.MESH
        )
    own_columns = pl.ds(pl.multiple_of(section * columns, columns), columns)
    local = [
        pltpu.make_async_copy(tok.at[:, own_columns], tbuf.at[section], local_sem.at[0]),
        pltpu.make_async_copy(fac, fbuf.at[section], local_sem.at[1]),
        pltpu.make_async_copy(
            w_into.at[:, own_columns], praw.at[section, pl.ds(0, hd)], local_sem.at[2]
        ),
        pltpu.make_async_copy(
            a_into.at[:, own_columns], praw.at[section, pl.ds(hd, rank)], local_sem.at[3]
        ),
        pltpu.make_async_copy(
            w_outof.at[:, own_columns], qbuf.at[section, pl.ds(0, hd)], local_sem.at[4]
        ),
        pltpu.make_async_copy(
            a_outof.at[:, own_columns], qbuf.at[section, pl.ds(hd, rank)], local_sem.at[5]
        ),
        pltpu.make_async_copy(gain_row.at[:, own_columns], gbuf.at[section], local_sem.at[6]),
    ]
    for copy in local:
        copy.start()
    pl.semaphore_wait(barrier, len(greeted))

    share_rows = pl.ds(pl.multiple_of(core * half, half), half)
    rank_rows = pl.ds(hd, rank)

    def to_columns(q):
        return pl.ds(pl.multiple_of(q * columns, columns), columns)

    def tok_copy(j, src_section):
        q = peers[j]
        return remote(
            tok.at[:, to_columns(q)], tbuf.at[src_section], tok_sem, j, (q, member), src_section
        )

    def fac_copy(j, src_section):
        return remote(fac, fbuf.at[src_section], fac_sem, j, (peers[j], member), src_section)

    def gain_copy(j, src_section):
        q = peers[j]
        return remote(
            gain_row.at[:, to_columns(q)],
            gbuf.at[src_section],
            gain_sem,
            j,
            (q, member),
            src_section,
        )

    def weight_copy(src, buf, sem):
        def copy_of(j, src_section):
            q = peers[j]
            return remote(
                src.at[share_rows, to_columns(q)],
                buf.at[src_section, share_rows],
                sem,
                j,
                (q, member),
                src_section,
            )

        return copy_of

    def adapter_copy(src, buf, sem):
        def copy_of(j, src_section):
            q = peers[j]
            return remote(
                src.at[:, to_columns(q)],
                buf.at[src_section, rank_rows],
                sem,
                j,
                (q, member),
                src_section,
            )

        return copy_of

    p_copy, pa_copy = weight_copy(w_into, praw, p_sem), adapter_copy(a_into, praw, pa_sem)
    q_copy, qa_copy = weight_copy(w_outof, qbuf, q_sem), adapter_copy(a_outof, qbuf, qa_sem)

    def sib_weight(buf, sem, layer):
        piece = buf.at[layer, share_rows]
        return remote(piece, piece, sem, layer, sibling)

    def arrive(copy_of, layer):
        @pl.when(section != layer)
        def _():
            copy_of(0, layer).wait_recv()

    def arrive_and_pass(copy_of, buf, sem, layer):
        @pl.when(section != layer)
        def _():
            copy_of(0, layer).wait_recv()
            sib_weight(buf, sem, layer).start()

    def passed(buf, sem, layer):
        @pl.when(section != layer)
        def _():
            sib_weight(buf, sem, layer).wait_recv()

    def block_rows(buf, at_level):
        start = pl.multiple_of((at_level * 2 + core) * block, block)
        return buf.at[pl.ds(start, block)]

    def up_copy(buf, sem, k):
        piece = block_rows(buf, level - k)
        return remote(piece, piece, sem, k, (section, member + 2))

    def down_copy(buf, sem, k):
        piece = block_rows(buf, level + k)
        return remote(piece, piece, sem, k, (section, member - 2))

    def sib_copy(buf, sem, at_level):
        piece = block_rows(buf, at_level)
        return remote(piece, piece, sem, at_level, sibling)

    def line_start(buf, up, down, k):
        @pl.when((level < levels - 1) & (level - k >= 0))
        def _():
            up_copy(buf, up, k).start()

        @pl.when((level > 0) & (level + k < levels))
        def _():
            down_copy(buf, down, k).start()

    def line_arrive(buf, up, down, sib, k):
        @pl.when(level - 1 - k >= 0)
        def _():
            up_copy(buf, up, k).wait_recv()

        @pl.when(level + 1 + k < levels)
        def _():
            down_copy(buf, down, k).wait_recv()

        if k + 1 < levels - 1:
            line_start(buf, up, down, k + 1)

        @pl.when(level - 1 - k >= 0)
        def _():
            sib_copy(buf, sib, level - 1 - k).start()

        @pl.when(level + 1 + k < levels)
        def _():
            sib_copy(buf, sib, level + 1 + k).start()

    def line_sent(buf, up, down, sib):
        for k in range(levels - 1):

            @pl.when((level < levels - 1) & (level - k >= 0))
            def _(k=k):
                up_copy(buf, up, k).wait_send()

            @pl.when((level > 0) & (level + k < levels))
            def _(k=k):
                down_copy(buf, down, k).wait_send()

        for at_level in range(levels):
            sib_copy(buf, sib, at_level).wait_send()

    def sum_copy(out, into, sem, layer, part, j):
        return remote(
            out.at[layer, part],
            into.at[layer, part, j],
            sem,
            (layer * 2 + part) * (sections - 1) + j,
            (peers[j], member),
        )

    def send_sum(out, into, sem, layer, part, partial):
        out[layer, part] = partial.astype(jnp.bfloat16)
        for j in range(sections - 1):
            sum_copy(out, into, sem, layer, part, j).start()

    def whole_sum(out, into, sem, layer, part, partial):
        for j in range(sections - 1):
            sum_copy(out, into, sem, layer, part, j).wait_recv()
        for j in range(sections - 1):
            partial = partial + into[layer, part, j].astype(jnp.float32)
        return partial

    for j in range(sections - 1):
        tok_copy(j, section).start()
    for j in range(sections - 1):
        p_copy(j, section).start()
        pa_copy(j, section).start()
        gain_copy(j, section).start()
        fac_copy(j, section).start()

    local[0].wait()
    for layer in range(sections):
        arrive(tok_copy, layer)
    per = block // sections
    for t in range(chunks):
        at = pl.ds(t * step, step)
        wide = [tbuf[m, :, at].astype(jnp.float32) for m in range(sections)]
        own = pl.ds(pl.multiple_of(member * block, block), block)
        hid[0, own, at] = jnp.concatenate([w[:per] for w in wide]).astype(jnp.bfloat16)
        cot[own, at] = jnp.concatenate([w[per:] for w in wide]).astype(jnp.bfloat16)
    x0 = hid.at[0]
    line_start(x0, x_up, x_down, 0)
    sib_copy(x0, x_sib, level).start()
    for j in range(sections - 1):
        q_copy(j, section).start()
        qa_copy(j, section).start()
    for copy in local[1:]:
        copy.wait()

    ones = jnp.ones((16, 128), jnp.bfloat16)

    def chunk(t):
        return pl.ds(pl.multiple_of(t * step, step), step)

    def project(layer, at, wide, rows):
        squares = wide * wide
        lanes = squares[:, :128]
        for start in range(128, step, 128):
            lanes = lanes + squares[:, start : start + 128]
        return trail(pbuf[layer, :, at], rows), lanes

    def add(left, right):
        return tuple(a + b for a, b in zip(left, right))

    zero_back = jnp.zeros((ranks, row_half), jnp.float32)
    zero_sum = (zero_back, jnp.zeros((row_half, 128), jnp.float32))

    def send_forward(layer, part, total):
        lanes = total[1]
        high = lanes.astype(jnp.bfloat16)
        low = (lanes - high.astype(jnp.float32)).astype(jnp.bfloat16)
        squares = (trail(ones, high) + trail(ones, low))[:8]
        high = squares.astype(jnp.bfloat16).astype(jnp.float32)
        partial = jnp.concatenate([total[0], high, squares - high])
        send_sum(fx_out, fx_in, fx_sem, layer, part, partial)
        return partial

    def turn(parts):
        parts = jnp.concatenate(parts)
        spare = jnp.zeros((128 - parts.shape[0], row_half), jnp.float32)
        return jnp.concatenate([parts, spare]).T

    def in_order(parts):
        wide = [part.astype(jnp.float32) for part in parts]
        straight, swapped = jnp.concatenate(wide, axis=1), jnp.concatenate(wide[::-1], axis=1)
        return jnp.where(near == 0, straight, swapped).astype(jnp.bfloat16)

    def fold(layer):
        passed(praw, psib_sem, layer)
        pbuf[layer] = (praw[layer].astype(jnp.float32) * gbuf[layer]).astype(jnp.bfloat16)

    def fold_rank(layer, raw, folded, top_by, low_by):
        def piece(t, carry):
            at = chunk(t)
            top = raw[layer, :hd, at].astype(jnp.float32)
            top = top + adapter_scale * plain(top_by, raw[layer, hd:, at])
            top = top.astype(jnp.bfloat16)
            folded[layer, :hd, at] = top
            folded[layer, hd:, at] = (adapter_scale * plain(low_by, top)).astype(jnp.bfloat16)
            return carry

        lax.fori_loop(0, chunks, piece, 0)

    def fold_into(layer):
        factor = fbuf[layer]
        fold_rank(layer, pbuf, pfold, factor[rank:, :rank], factor[:rank, hd : 2 * hd])

    def fold_outof(layer):
        factor = fbuf[layer]
        fold_rank(layer, qbuf, qfold, factor[rank:, hd : hd + rank], factor[:rank, :hd])

    def take_first(part):
        def first(t, total):
            rows = hid[0, half_rows[part], chunk(t)]
            return add(total, project(0, chunk(t), rows.astype(jnp.float32), rows))

        return send_forward(0, part, lax.fori_loop(0, chunks, first, zero_sum, unroll=True))

    def line_levels(buf, sib, wanted):
        for at_level in range(levels):

            @pl.when((lax.div(at_level, levels // 2) == lax.div(level, levels // 2)) == wanted)
            def _(at_level=at_level):
                sib_copy(buf, sib, at_level).wait_recv()

    reach = levels // 2 - 1
    for k in range(reach):
        line_arrive(x0, x_up, x_down, x_sib, k)
    for layer in range(sections):
        arrive_and_pass(p_copy, praw, psib_sem, layer)
        arrive(pa_copy, layer)
        arrive(gain_copy, layer)
        arrive(fac_copy, layer)
    fold(0)
    line_levels(x0, x_sib, True)
    partials = [take_first(0)]
    for k in range(reach, levels - 1):
        line_arrive(x0, x_up, x_down, x_sib, k)
    line_start(cot, c_up, c_down, 0)
    sib_copy(cot, c_sib, level).start()
    line_levels(x0, x_sib, False)
    partials.append(take_first(1))

    last = sections - 1
    kept, sides, backs = [], [], [None, None]
    for layer in range(sections):
        if layer == 0:
            for later in range(1, sections):
                fold(later)
                fold_into(later)
            arrive_and_pass(q_copy, qbuf, qsib_sem, 0)
            arrive(qa_copy, 0)
        if layer == 1:
            for later in range(1, sections):
                arrive_and_pass(q_copy, qbuf, qsib_sem, later)
                arrive(qa_copy, later)
        if layer < levels - 1:
            line_arrive(cot, c_up, c_down, c_sib, layer)
        passed(qbuf, qsib_sem, layer)
        if layer < last:
            fold_outof(layer)
        if layer == last:
            for k in range(last + 1, levels - 1):
                line_arrive(cot, c_up, c_down, c_sib, k)
            for at_level in range(levels):
                sib_copy(cot, c_sib, at_level).wait_recv()
            for part in range(2):
                rows_of = half_rows[part]

                def seed(t, total_now, rows_of=rows_of):
                    at = chunk(t)
                    top = cot[rows_of, at].astype(jnp.float32) * row_weight[rows_of, :]
                    top = top.astype(jnp.bfloat16)
                    grad[last, rows_of, at] = top
                    return total_now + trail(qbuf[last, :, at], top)

                backs[part] = lax.fori_loop(0, chunks, seed, zero_back, unroll=True)
                send_sum(bx_out, bx_in, bx_sem, last, part, backs[part])
        factor = fbuf[layer]
        halves = []
        for part in range(2):
            rows_of = half_rows[part]
            whole = whole_sum(fx_out, fx_in, fx_sem, layer, part, partials[part])
            projection = whole[:ranks]
            squares = whole[ranks : ranks + 1] + whole[ranks + 8 : ranks + 9]
            inverse = lax.rsqrt(squares / width + norm_eps)
            scaled = projection * inverse
            halves.append((scaled, inverse))
            if layer < last:
                turned[part] = turn([scaled]).astype(jnp.bfloat16)

                def update(t, total_now, layer=layer, part=part, rows_of=rows_of):
                    at = chunk(t)
                    rows = hid[layer, rows_of, at].astype(jnp.float32)
                    rows = rows + plain(turned[part, :, :ranks], qfold[layer, :, at])
                    rows = rows.astype(jnp.bfloat16)
                    hid[layer + 1, rows_of, at] = rows
                    return add(
                        total_now, project(layer + 1, at, rows.astype(jnp.float32), rows)
                    )

                total = lax.fori_loop(0, chunks, update, zero_sum, unroll=True)
                partials[part] = send_forward(layer + 1, part, total)
        smalls = []
        for scaled, inverse in halves:
            lowrank = scaled[hd:].astype(jnp.bfloat16)
            value = (
                scaled[:hd] + adapter_scale * plain(factor[rank:, :rank], lowrank)
            ).astype(jnp.bfloat16)
            side = plain(factor[:rank, hd : 2 * hd], value).astype(jnp.bfloat16)
            mixed = jnp.concatenate(
                [value.astype(jnp.float32), adapter_scale * side.astype(jnp.float32)]
            )
            smalls.append((mixed, inverse, lowrank, value, side))
        kept.append(smalls)
        sides.append(in_order([h[4] for h in smalls]))

    def land_copy(layer, which):
        return remote(
            mine.at[layer, which],
            land.at[section, which],
            land_sem,
            layer * 2 + which,
            (layer, member),
            section * 2 + which,
        )

    def collect(layer, which, small, wide, by):
        def gather(t, carry):
            at = chunk(t)
            mine[layer, which, :, at] = (by * plain(small, wide[layer, :, at])).astype(
                jnp.bfloat16
            )
            return carry

        lax.fori_loop(0, chunks, gather, 0, unroll=True)

        @pl.when(section != layer)
        def _():
            land_copy(layer, which).start()

        @pl.when(section == layer)
        def _():
            land[layer, which] = mine[layer, which]

    collect(last, 1, sides[last], grad, adapter_scale)
    for layer in reversed(range(sections)):
        factor = fbuf[layer]
        lows, small_up, small_down = [], None, None
        wholes = []
        for part in range(2):
            rows_of = half_rows[part]
            mixed, inverse = kept[layer][part][:2]
            whole = whole_sum(bx_out, bx_in, bx_sem, layer, part, backs[part])
            wholes.append(whole)
            if layer > 0:
                correction = jnp.sum(whole * mixed, axis=0, keepdims=True) / width
                shrink = jnp.broadcast_to(inverse * inverse * correction, (8, row_half))
                columns_of = turn([whole * inverse, shrink])
                turned[part] = columns_of.astype(jnp.bfloat16)
                shrink_column = columns_of[:, ranks : ranks + 1]

                def step_back(
                    t, total_now, layer=layer, part=part, rows_of=rows_of, shrink=shrink_column
                ):
                    at = chunk(t)
                    rows = hid[layer, rows_of, at].astype(jnp.float32)
                    fresh = grad[layer, rows_of, at].astype(jnp.float32)
                    fresh = fresh + plain(turned[part, :, :ranks], pfold[layer, :, at])
                    fresh = (fresh - rows * shrink).astype(jnp.bfloat16)
                    grad[layer - 1, rows_of, at] = fresh
                    return total_now + trail(qbuf[layer - 1, :, at], fresh)

                backs[part] = lax.fori_loop(0, chunks, step_back, zero_back, unroll=True)
                send_sum(bx_out, bx_in, bx_sem, layer - 1, part, backs[part])
        for whole, (mixed, inverse, lowrank, value, side) in zip(wholes, kept[layer]):
            grad_side = (adapter_scale * whole[hd:]).astype(jnp.bfloat16)
            grad_value = (whole[:hd] + plain(factor[rank:, hd : hd + rank], grad_side)).astype(
                jnp.bfloat16
            )
            grad_low = (adapter_scale * plain(factor[:rank, :hd], grad_value)).astype(
                jnp.bfloat16
            )
            lows.append(grad_low.astype(jnp.float32) * inverse)
            up_now = trail(lowrank, grad_value)
            down_now = trail(grad_side, value)
            small_up = up_now if small_up is None else small_up + up_now
            small_down = down_now if small_down is None else small_down + down_now
        collect(layer, 0, in_order(lows), hid, 1.0)
        if layer > 0:
            collect(layer - 1, 1, sides[layer - 1], grad, adapter_scale)

        @pl.when(section == layer)
        def _(small_up=small_up, small_down=small_down):
            out_vu[...] = (adapter_scale * small_up).astype(jnp.bfloat16)
            out_od[...] = small_down.astype(jnp.bfloat16)

    def landed(source, which):
        @pl.when(section != source)
        def _():
            remote(
                mine.at[source, which],
                land.at[source, which],
                land_sem,
                source * 2 + which,
                (source, member),
                source * 2 + which,
            ).wait()

    for q in range(sections):
        landed(q, 1)
        at = pl.ds(q * columns, columns)
        out_ou[:, at] = land[q, 1]
    for j in range(sections - 1):
        for copy_of in (tok_copy, fac_copy, gain_copy, p_copy, pa_copy, q_copy, qa_copy):
            copy_of(j, section).wait_send()
        for layer in range(sections):
            for part in range(2):
                sum_copy(fx_out, fx_in, fx_sem, layer, part, j).wait_send()
                sum_copy(bx_out, bx_in, bx_sem, layer, part, j).wait_send()
    for layer in range(sections):

        @pl.when(section != layer)
        def _(layer=layer):
            sib_weight(praw, psib_sem, layer).wait_send()
            sib_weight(qbuf, qsib_sem, layer).wait_send()

    line_sent(x0, x_up, x_down, x_sib)
    line_sent(cot, c_up, c_down, c_sib)
    for q in range(sections):
        landed(q, 0)
        at = pl.ds(q * columns, columns)
        out_vd[:, at] = (land[q, 0].astype(jnp.float32) * gain[:, at]).astype(jnp.bfloat16)


def kernel_body(
    inputs,
    cotangent,
    norm_gain,
    w_value,
    w_out,
    value_down,
    value_up_factor,
    out_down,
    output_up_factor,
    block_tenant,
    valid_tokens,
    tenant_slot,
):
    sections, members = lax.axis_size("pipe"), lax.axis_size("dp")
    member = lax.axis_index("dp")
    row_count, width = inputs.shape[1:]
    micro_count = inputs.shape[0] * sections
    columns, row_total = width // sections, micro_count * row_count * members
    rank, hd = value_up_factor.shape[2:]
    ranks, row_half = hd + rank, row_total // 2
    tok = jnp.concatenate([inputs[0], cotangent[0]])
    up, down = value_up_factor[0, 0], out_down[0, 0]
    pad = ((0, 0), (0, hd - rank))
    fac = jnp.concatenate(
        [
            jnp.concatenate([up, down], axis=1),
            jnp.concatenate([jnp.pad(up.T, pad), jnp.pad(down.T, pad)], axis=1),
        ]
    )
    weight = row_weights(
        block_tenant, valid_tokens, tenant_slot, member, micro_count, row_count
    ).reshape(-1, 1)
    half_type, levels = jnp.bfloat16, members // 2
    dma = pltpu.SemaphoreType.DMA
    vmem, anywhere = pl.BlockSpec(memory_space=pltpu.VMEM), pl.BlockSpec(memory_space=pl.ANY)
    sums = sections * (sections - 1)
    outs = pl.pallas_call(
        functools.partial(columns_kernel, (sections, members)),
        out_shape=(
            jax.ShapeDtypeStruct((rank, width), half_type),
            jax.ShapeDtypeStruct((rank, hd), half_type),
            jax.ShapeDtypeStruct((rank, hd), half_type),
            jax.ShapeDtypeStruct((rank, width), half_type),
        ),
        in_specs=[anywhere] * 7 + [vmem, vmem],
        out_specs=(vmem, vmem, vmem, vmem),
        scratch_shapes=[
            pltpu.VMEM((sections, row_total, columns), half_type),
            pltpu.VMEM((sections, row_total, columns), half_type),
            pltpu.VMEM((row_total, columns), half_type),
            pltpu.VMEM((sections, 2 * row_count, columns), half_type),
            pltpu.VMEM((sections, ranks, columns), half_type),
            pltpu.VMEM((sections, ranks, columns), half_type),
            pltpu.VMEM((sections, ranks, columns), half_type),
            pltpu.VMEM((sections, ranks, columns), half_type),
            pltpu.VMEM((sections, ranks, columns), half_type),
            pltpu.VMEM((sections,) + fac.shape, half_type),
            pltpu.VMEM((sections, 1, columns), jnp.float32),
            pltpu.VMEM((2, row_half, 128), half_type),
            pltpu.VMEM((sections, 2, rank, columns), half_type),
            pltpu.VMEM((sections, 2, rank, columns), half_type),
            pltpu.VMEM((sections, 2, ranks + 16, row_half), half_type),
            pltpu.VMEM((sections, 2, sections - 1, ranks + 16, row_half), half_type),
            pltpu.VMEM((sections, 2, ranks, row_half), half_type),
            pltpu.VMEM((sections, 2, sections - 1, ranks, row_half), half_type),
            dma((7,)),
            dma((2, sections)),
            dma((2, sections)),
            dma((2, sections)),
            dma((2, sections)),
            dma((2, sections)),
            dma((2, sections)),
            dma((2, sections)),
            dma((2, sections)),
            dma((2, sections)),
            dma((2, levels)),
            dma((2, levels)),
            dma((2, levels)),
            dma((2, levels)),
            dma((2, levels)),
            dma((2, levels)),
            dma((2, 2 * sums)),
            dma((2, 2 * sums)),
            dma((2, 2 * sections)),
        ],
        compiler_params=pltpu.CompilerParams(
            collective_id=0, has_side_effects=True, vmem_limit_bytes=60 * 2**20
        ),
    )(
        tok,
        w_value[0],
        value_down[0, 0],
        w_out[0],
        output_up_factor[0, 0],
        norm_gain,
        fac,
        weight,
        norm_gain,
    )
    return tuple(part[None, None] for part in outs)


def solution(mesh):
    sections = mesh.shape["pipe"]

    def run(*arrays):
        depth, row_total, width = arrays[0].shape
        kept_bytes = 2 * depth * row_total * (width // sections) * sections
        chosen = kernel_body if kept_bytes <= stash_limit else relay_body
        return place(chosen)(*arrays)

    def place(chosen):
        return jax.shard_map(
            chosen,
            mesh=mesh,
            in_specs=(
                P("pipe", "dp", None),
                P("pipe", "dp", None),
                P("pipe", None),
                P("pipe", None, None),
                P("pipe", None, None),
                P("pipe", "dp", None, None),
                P("pipe", "dp", None, None),
                P("pipe", "dp", None, None),
                P("pipe", "dp", None, None),
                P(),
                P(),
                P(),
            ),
            out_specs=(
                P("pipe", "dp", None, None),
                P("pipe", "dp", None, None),
                P("pipe", "dp", None, None),
                P("pipe", "dp", None, None),
            ),
            check_vma=False,
        )

    return run
```

```python
import functools

import jax
import jax.numpy as jnp
from jax import lax
from jax.experimental import pallas as pl
from jax.experimental.pallas import tpu as pltpu
from jax.sharding import PartitionSpec as P

adapter_scale = 2.0
norm_eps = 1e-05
stash_limit = 8 * 2**20


def from_behind(value, axis, by):
    peers = lax.axis_size(axis)
    return lax.ppermute(value, axis, [(i, (i + by) % peers) for i in range(peers)])


def normalize(token_rows, gain_row):
    wide_rows = token_rows.astype(jnp.float32)
    inverse = lax.rsqrt(jnp.mean(wide_rows * wide_rows, axis=-1, keepdims=True) + norm_eps)
    return ((wide_rows * inverse * gain_row).astype(jnp.bfloat16), inverse)


def contract_trailing(left, right):
    return lax.dot_general(
        left, right, (((1,), (1,)), ((), ())), preferred_element_type=jnp.float32
    )


def contract_leading(left, right):
    return lax.dot_general(
        left, right, (((0,), (0,)), ((), ())), preferred_element_type=jnp.float32
    )


def section_parts(token_rows, gain_row, value_weight, tenant_adapters):
    value_down, value_up_factor, out_down, output_up_factor = tenant_adapters
    normalized_rows, inverse = normalize(token_rows, gain_row)
    lowrank_product = contract_trailing(normalized_rows, value_down).astype(jnp.bfloat16)
    value_blend = contract_trailing(normalized_rows, value_weight)
    value_blend = value_blend + adapter_scale * jnp.dot(
        lowrank_product, value_up_factor, preferred_element_type=jnp.float32
    )
    value_row_block = value_blend.astype(jnp.bfloat16)
    sidepath_rank = contract_trailing(value_row_block, out_down).astype(jnp.bfloat16)
    return (normalized_rows, inverse, lowrank_product, value_row_block, sidepath_rank)


def section_output(token_rows, layer_pieces, out_weight, tenant_adapters):
    blended_rows = token_rows.astype(jnp.float32) + jnp.dot(
        layer_pieces[3], out_weight, preferred_element_type=jnp.float32
    )
    blended_rows = blended_rows + adapter_scale * jnp.dot(
        layer_pieces[4], tenant_adapters[3], preferred_element_type=jnp.float32
    )
    return blended_rows.astype(jnp.bfloat16)


def section_backward(
    token_rows, input_gradient, layer_pieces, gain_row, value_weight, out_weight, tenant_adapters
):
    value_down, value_up_factor, out_down, output_up_factor = tenant_adapters
    normalized_rows, inverse, lowrank_product, value_row_block, sidepath_rank = layer_pieces
    sidepath_gradient = (
        adapter_scale * contract_trailing(input_gradient, output_up_factor)
    ).astype(jnp.bfloat16)
    value_gradient = contract_trailing(input_gradient, out_weight)
    value_gradient = (
        value_gradient + jnp.dot(sidepath_gradient, out_down, preferred_element_type=jnp.float32)
    ).astype(jnp.bfloat16)
    lowrank_gradient = (adapter_scale * contract_trailing(value_gradient, value_up_factor)).astype(
        jnp.bfloat16
    )
    grad_normed = jnp.dot(
        value_gradient, value_weight, preferred_element_type=jnp.float32
    ) + jnp.dot(lowrank_gradient, value_down, preferred_element_type=jnp.float32)
    scaled = grad_normed * gain_row
    wide_rows = token_rows.astype(jnp.float32)
    correction = jnp.mean(scaled * wide_rows, axis=-1, keepdims=True)
    grad_rows = inverse * scaled - wide_rows * (inverse * inverse * inverse) * correction
    grad_out = (input_gradient.astype(jnp.float32) + grad_rows).astype(jnp.bfloat16)
    gradient_pieces = (
        contract_leading(lowrank_gradient, normalized_rows),
        adapter_scale * contract_leading(lowrank_product, value_gradient),
        contract_leading(sidepath_gradient, value_row_block),
        adapter_scale * contract_leading(sidepath_rank, input_gradient),
    )
    return (grad_out, gradient_pieces)


def pass_section(token_rows, shift_by):
    return from_behind(token_rows, "pipe", shift_by)


def owner_layout(first, second, third, fourth):
    return (
        lax.all_to_all(first, "dp", split_axis=0, concat_axis=2, tiled=True),
        lax.all_to_all(second, "dp", split_axis=0, concat_axis=2, tiled=True),
        lax.all_to_all(third, "dp", split_axis=0, concat_axis=2, tiled=True),
        lax.all_to_all(fourth, "dp", split_axis=0, concat_axis=2, tiled=True),
    )


def pick_rows(picker, sliced_part):
    flat_rows = sliced_part.reshape(sliced_part.shape[0], -1)
    chosen = jnp.dot(picker, flat_rows, preferred_element_type=jnp.float32).astype(jnp.bfloat16)
    return chosen.reshape((picker.shape[0],) + sliced_part.shape[1:])


def sum_by_slot(slot_float, gathered_part):
    flat_rows = gathered_part.reshape(gathered_part.shape[0], -1)
    summed = lax.dot_general(
        slot_float,
        flat_rows,
        (((0,), (0,)), ((), ())),
        precision=lax.Precision.HIGHEST,
        preferred_element_type=jnp.float32,
    )
    return summed.astype(jnp.bfloat16).reshape((slot_float.shape[1],) + gathered_part.shape[1:])


def put_entry(stash, entry, micro_index, active):

    def update(stored_all, new_entry):
        previous = lax.dynamic_index_in_dim(stored_all, micro_index, 0, keepdims=False)
        return lax.dynamic_update_index_in_dim(
            stored_all, jnp.where(active, new_entry, previous), micro_index, 0
        )

    return jax.tree.map(update, stash, entry)


def get_entry(stash, micro_index):
    return jax.tree.map(
        lambda stored_all: lax.dynamic_index_in_dim(stored_all, micro_index, 0, keepdims=False),
        stash,
    )


def relay_body(
    inputs,
    cotangent,
    norm_gain,
    w_value,
    w_out,
    value_down,
    value_up_factor,
    out_down,
    output_up_factor,
    block_tenant,
    valid_tokens,
    tenant_slot,
):
    section_index = lax.axis_index("pipe")
    sections = lax.axis_size("pipe")
    member = lax.axis_index("dp")
    members = lax.axis_size("dp")
    queue_depth = inputs.shape[0]
    row_count = inputs.shape[1]
    micro_count = queue_depth * sections
    ticks = micro_count + sections - 1
    tenant_ids = jnp.arange(tenant_slot.shape[0], dtype=jnp.int32)
    tenant_hot = block_tenant[:, None] == tenant_ids[None, :]
    slot_of = jnp.sum(jnp.where(tenant_hot, tenant_slot[None, :], 0), axis=1)
    slot_hot = slot_of[:, None] == tenant_ids[None, :]
    member_hot = jnp.arange(members, dtype=jnp.int32) == member
    own_tenant = jnp.sum(jnp.where(member_hot, block_tenant, 0))
    own_valid = jnp.sum(jnp.where(member_hot, valid_tokens, 0))
    tenant_tokens = jnp.sum(jnp.where(block_tenant == own_tenant, valid_tokens, 0)).astype(
        jnp.float32
    )
    sliced = (
        lax.all_to_all(value_down[0], "dp", split_axis=2, concat_axis=0, tiled=True),
        lax.all_to_all(value_up_factor[0], "dp", split_axis=2, concat_axis=0, tiled=True),
        lax.all_to_all(out_down[0], "dp", split_axis=2, concat_axis=0, tiled=True),
        lax.all_to_all(output_up_factor[0], "dp", split_axis=2, concat_axis=0, tiled=True),
    )
    picker = slot_hot.astype(jnp.bfloat16)
    picked = [pick_rows(picker, sliced_part) for sliced_part in sliced]
    fetched = owner_layout(picked[0], picked[1], picked[2], picked[3])
    tenant_adapters = tuple((whole_part[0] for whole_part in fetched))
    gain_row = norm_gain[0]
    value_weight = w_value[0]
    out_weight = w_out[0]

    def token_weight(micro_index):
        position = micro_index * row_count + jnp.arange(row_count, dtype=jnp.int32)
        return (
            jnp.where(position < own_valid, 1.0, 0.0).astype(jnp.float32)[:, None] / tenant_tokens
        )

    def keep_entry(current):
        return (current,)

    def parts_of(entry):
        return section_parts(entry[0], gain_row, value_weight, tenant_adapters)

    blank = jnp.zeros((row_count, inputs.shape[2]), jnp.bfloat16)
    sample = keep_entry(blank)
    stash = jax.tree.map(
        lambda leaf_value: jnp.zeros((micro_count,) + leaf_value.shape, leaf_value.dtype), sample
    )
    accum = tuple((jnp.zeros(adapter_part.shape, jnp.float32) for adapter_part in tenant_adapters))

    def forward_tick(tick_index, arriving, feed_rows, stash_now, order):
        position = tick_index - section_index
        active = (position >= 0) & (position < micro_count)
        micro_index = order(jnp.clip(position, 0, micro_count - 1))
        current = jnp.where(section_index == 0, feed_rows, arriving)
        layer_pieces = section_parts(current, gain_row, value_weight, tenant_adapters)
        result = section_output(current, layer_pieces, out_weight, tenant_adapters)
        stash_now = put_entry(stash_now, keep_entry(current), micro_index, active)
        return (result, stash_now)

    def backward_tick(tick_index, arriving, feed_rows, stash_now, accum_now, order):
        position = tick_index - (sections - 1 - section_index)
        active = (position >= 0) & (position < micro_count)
        micro_index = order(jnp.clip(position, 0, micro_count - 1))
        entry = get_entry(stash_now, micro_index)
        seeded = (feed_rows.astype(jnp.float32) * token_weight(micro_index)).astype(jnp.bfloat16)
        input_gradient = jnp.where(section_index == sections - 1, seeded, arriving)
        grad_out, gradient_pieces = section_backward(
            entry[0],
            input_gradient,
            parts_of(entry),
            gain_row,
            value_weight,
            out_weight,
            tenant_adapters,
        )
        accum_now = tuple(
            (
                running + jnp.where(active, addend, 0.0)
                for running, addend in zip(accum_now, gradient_pieces)
            )
        )
        return (grad_out, accum_now)

    all_inputs, all_cotangents = (
        lax.all_gather(inputs, "pipe", axis=0, tiled=True),
        lax.all_gather(cotangent, "pipe", axis=0, tiled=True),
    )

    def plain_order(position):
        return position

    def forward_step(tick_index, carry):
        arriving, stash_now = carry
        feed_rows = lax.dynamic_index_in_dim(
            all_inputs, jnp.minimum(tick_index, micro_count - 1), 0, keepdims=False
        )
        result, stash_now = forward_tick(tick_index, arriving, feed_rows, stash_now, plain_order)
        return (pass_section(result, 1), stash_now)

    arriving, stash = lax.fori_loop(0, ticks, forward_step, (blank, stash))

    def backward_step(tick_index, carry):
        arriving, accum_now = carry
        feed_rows = lax.dynamic_index_in_dim(
            all_cotangents, jnp.minimum(tick_index, micro_count - 1), 0, keepdims=False
        )
        grad_out, accum_now = backward_tick(
            tick_index, arriving, feed_rows, stash, accum_now, plain_order
        )
        return (pass_section(grad_out, sections - 1), accum_now)

    arriving, accum = lax.fori_loop(0, ticks, backward_step, (blank, accum))
    spread = (
        lax.all_to_all(
            accum[0][None].astype(jnp.bfloat16), "dp", split_axis=2, concat_axis=0, tiled=True
        ).astype(jnp.float32),
        lax.all_to_all(
            accum[1][None].astype(jnp.bfloat16), "dp", split_axis=2, concat_axis=0, tiled=True
        ).astype(jnp.float32),
        lax.all_to_all(
            accum[2][None].astype(jnp.bfloat16), "dp", split_axis=2, concat_axis=0, tiled=True
        ).astype(jnp.float32),
        lax.all_to_all(
            accum[3][None].astype(jnp.bfloat16), "dp", split_axis=2, concat_axis=0, tiled=True
        ).astype(jnp.float32),
    )
    slot_float = slot_hot.astype(jnp.float32)
    totals = [sum_by_slot(slot_float, gathered_part) for gathered_part in spread]
    owned = owner_layout(totals[0], totals[1], totals[2], totals[3])
    return (owned[0][None], owned[1][None], owned[2][None], owned[3][None])


def trail(left, right):
    return lax.dot_general(
        left, right, (((1,), (1,)), ((), ())), preferred_element_type=jnp.float32
    )


def plain(left, right):
    return jnp.dot(left, right, preferred_element_type=jnp.float32)


def row_weights(block_tenant, valid_tokens, tenant_slot, member, micro_count, row_count):
    tenant_ids = jnp.arange(tenant_slot.shape[0], dtype=jnp.int32)
    tenant_hot = block_tenant[:, None] == tenant_ids[None, :]
    slot_of = jnp.sum(jnp.where(tenant_hot, tenant_slot[None, :], 0), axis=1)
    same = block_tenant[:, None] == block_tenant[None, :]
    tokens = jnp.sum(jnp.where(same, valid_tokens[None, :], 0), axis=1).astype(jnp.float32)
    position = jnp.arange(micro_count * row_count, dtype=jnp.int32)
    keep = (position[None, :] < valid_tokens[:, None]) & (slot_of[:, None] == member)
    return jnp.where(keep, 1.0, 0.0).astype(jnp.float32) / tokens[:, None]


def columns_kernel(
    shape,
    tok,
    w_into,
    a_into,
    w_outof,
    a_outof,
    gain_row,
    fac,
    row_weight,
    gain,
    out_vd,
    out_vu,
    out_od,
    out_ou,
    hid,
    grad,
    cot,
    tbuf,
    praw,
    pbuf,
    qbuf,
    pfold,
    fbuf,
    gbuf,
    turned,
    land,
    mine,
    fx_out,
    fx_in,
    bx_out,
    bx_in,
    local_sem,
    tok_sem,
    fac_sem,
    gain_sem,
    p_sem,
    pa_sem,
    q_sem,
    qa_sem,
    psib_sem,
    qsib_sem,
    x_up,
    x_down,
    x_sib,
    c_up,
    c_down,
    c_sib,
    fx_sem,
    bx_sem,
    land_sem,
):
    sections, members = shape
    levels = members // 2
    section, member = lax.axis_index("pipe"), lax.axis_index("dp")
    core, level = lax.rem(member, 2), lax.div(member, 2)
    sibling = (section, member + 1 - 2 * core)
    row_total, columns = hid.shape[1:]
    block = row_total // members
    width = columns * sections
    rank, hd = out_vu.shape
    half, ranks = hd // 2, hd + rank
    row_half = row_total // 2
    near = lax.div(level, levels // 2) * row_half
    half_rows = [
        pl.ds(pl.multiple_of(near, row_half), row_half),
        pl.ds(pl.multiple_of(row_half - near, row_half), row_half),
    ]
    peers = [lax.rem(section + j, sections) for j in range(1, sections)]
    step = min(512, columns)
    chunks = columns // step

    def remote(src, dst, sem, slot, target, got=None):
        return pltpu.make_async_remote_copy(
            src_ref=src,
            dst_ref=dst,
            send_sem=sem.at[0, slot],
            recv_sem=sem.at[1, slot if got is None else got],
            device_id=target,
            device_id_type=pl.DeviceIdType.MESH,
        )

    barrier = pltpu.get_barrier_semaphore()
    greeted = [(q, member) for q in peers] + [sibling]
    greeted += [(section, lax.rem(member + by, members)) for by in (2, members - 2)]
    for target in greeted:
        pl.semaphore_signal(
            barrier, inc=1, device_id=target, device_id_type=pl.DeviceIdType.MESH
        )
    own_columns = pl.ds(pl.multiple_of(section * columns, columns), columns)
    local = [
        pltpu.make_async_copy(tok.at[:, own_columns], tbuf.at[section], local_sem.at[0]),
        pltpu.make_async_copy(fac, fbuf.at[section], local_sem.at[1]),
        pltpu.make_async_copy(
            w_into.at[:, own_columns], praw.at[section, pl.ds(0, hd)], local_sem.at[2]
        ),
        pltpu.make_async_copy(
            a_into.at[:, own_columns], praw.at[section, pl.ds(hd, rank)], local_sem.at[3]
        ),
        pltpu.make_async_copy(
            w_outof.at[:, own_columns], qbuf.at[section, pl.ds(0, hd)], local_sem.at[4]
        ),
        pltpu.make_async_copy(
            a_outof.at[:, own_columns], qbuf.at[section, pl.ds(hd, rank)], local_sem.at[5]
        ),
        pltpu.make_async_copy(gain_row.at[:, own_columns], gbuf.at[section], local_sem.at[6]),
    ]
    for copy in local:
        copy.start()
    pl.semaphore_wait(barrier, len(greeted))

    share_rows = pl.ds(pl.multiple_of(core * half, half), half)
    rank_rows = pl.ds(hd, rank)

    def to_columns(q):
        return pl.ds(pl.multiple_of(q * columns, columns), columns)

    def tok_copy(j, src_section):
        q = peers[j]
        return remote(
            tok.at[:, to_columns(q)], tbuf.at[src_section], tok_sem, j, (q, member), src_section
        )

    def fac_copy(j, src_section):
        return remote(fac, fbuf.at[src_section], fac_sem, j, (peers[j], member), src_section)

    def gain_copy(j, src_section):
        q = peers[j]
        return remote(
            gain_row.at[:, to_columns(q)],
            gbuf.at[src_section],
            gain_sem,
            j,
            (q, member),
            src_section,
        )

    def weight_copy(src, buf, sem):
        def copy_of(j, src_section):
            q = peers[j]
            return remote(
                src.at[share_rows, to_columns(q)],
                buf.at[src_section, share_rows],
                sem,
                j,
                (q, member),
                src_section,
            )

        return copy_of

    def adapter_copy(src, buf, sem):
        def copy_of(j, src_section):
            q = peers[j]
            return remote(
                src.at[:, to_columns(q)],
                buf.at[src_section, rank_rows],
                sem,
                j,
                (q, member),
                src_section,
            )

        return copy_of

    p_copy, pa_copy = weight_copy(w_into, praw, p_sem), adapter_copy(a_into, praw, pa_sem)
    q_copy, qa_copy = weight_copy(w_outof, qbuf, q_sem), adapter_copy(a_outof, qbuf, qa_sem)

    def sib_weight(buf, sem, layer):
        piece = buf.at[layer, share_rows]
        return remote(piece, piece, sem, layer, sibling)

    def arrive(copy_of, layer):
        @pl.when(section != layer)
        def _():
            copy_of(0, layer).wait_recv()

    def arrive_and_pass(copy_of, buf, sem, layer):
        @pl.when(section != layer)
        def _():
            copy_of(0, layer).wait_recv()
            sib_weight(buf, sem, layer).start()

    def passed(buf, sem, layer):
        @pl.when(section != layer)
        def _():
            sib_weight(buf, sem, layer).wait_recv()

    def block_rows(buf, at_level):
        start = pl.multiple_of((at_level * 2 + core) * block, block)
        return buf.at[pl.ds(start, block)]

    def up_copy(buf, sem, k):
        piece = block_rows(buf, level - k)
        return remote(piece, piece, sem, k, (section, member + 2))

    def down_copy(buf, sem, k):
        piece = block_rows(buf, level + k)
        return remote(piece, piece, sem, k, (section, member - 2))

    def sib_copy(buf, sem, at_level):
        piece = block_rows(buf, at_level)
        return remote(piece, piece, sem, at_level, sibling)

    def line_start(buf, up, down, k):
        @pl.when((level < levels - 1) & (level - k >= 0))
        def _():
            up_copy(buf, up, k).start()

        @pl.when((level > 0) & (level + k < levels))
        def _():
            down_copy(buf, down, k).start()

    def line_arrive(buf, up, down, sib, k):
        @pl.when(level - 1 - k >= 0)
        def _():
            up_copy(buf, up, k).wait_recv()

        @pl.when(level + 1 + k < levels)
        def _():
            down_copy(buf, down, k).wait_recv()

        if k + 1 < levels - 1:
            line_start(buf, up, down, k + 1)

        @pl.when(level - 1 - k >= 0)
        def _():
            sib_copy(buf, sib, level - 1 - k).start()

        @pl.when(level + 1 + k < levels)
        def _():
            sib_copy(buf, sib, level + 1 + k).start()

    def line_sent(buf, up, down, sib):
        for k in range(levels - 1):

            @pl.when((level < levels - 1) & (level - k >= 0))
            def _(k=k):
                up_copy(buf, up, k).wait_send()

            @pl.when((level > 0) & (level + k < levels))
            def _(k=k):
                down_copy(buf, down, k).wait_send()

        for at_level in range(levels):
            sib_copy(buf, sib, at_level).wait_send()

    def sum_copy(out, into, sem, layer, part, j):
        return remote(
            out.at[layer, part],
            into.at[layer, part, j],
            sem,
            (layer * 2 + part) * (sections - 1) + j,
            (peers[j], member),
        )

    def send_sum(out, into, sem, layer, part, partial):
        out[layer, part] = partial.astype(jnp.bfloat16)
        for j in range(sections - 1):
            sum_copy(out, into, sem, layer, part, j).start()

    def whole_sum(out, into, sem, layer, part, partial):
        for j in range(sections - 1):
            sum_copy(out, into, sem, layer, part, j).wait_recv()
        for j in range(sections - 1):
            partial = partial + into[layer, part, j].astype(jnp.float32)
        return partial

    for j in range(sections - 1):
        tok_copy(j, section).start()
    for j in range(sections - 1):
        p_copy(j, section).start()
        pa_copy(j, section).start()
        gain_copy(j, section).start()
        fac_copy(j, section).start()

    local[0].wait()
    for layer in range(sections):
        arrive(tok_copy, layer)
    per = block // sections
    for t in range(chunks):
        at = pl.ds(t * step, step)
        wide = [tbuf[m, :, at].astype(jnp.float32) for m in range(sections)]
        own = pl.ds(pl.multiple_of(member * block, block), block)
        hid[0, own, at] = jnp.concatenate([w[:per] for w in wide]).astype(jnp.bfloat16)
        cot[own, at] = jnp.concatenate([w[per:] for w in wide]).astype(jnp.bfloat16)
    x0 = hid.at[0]
    line_start(x0, x_up, x_down, 0)
    sib_copy(x0, x_sib, level).start()
    for j in range(sections - 1):
        q_copy(j, section).start()
        qa_copy(j, section).start()
    for copy in local[1:]:
        copy.wait()

    ones = jnp.ones((16, 128), jnp.bfloat16)

    def chunk(t):
        return pl.ds(pl.multiple_of(t * step, step), step)

    def project(layer, at, wide, rows):
        squares = wide * wide
        lanes = squares[:, :128]
        for start in range(128, step, 128):
            lanes = lanes + squares[:, start : start + 128]
        return trail(pbuf[layer, :, at], rows), lanes

    def add(left, right):
        return tuple(a + b for a, b in zip(left, right))

    zero_back = jnp.zeros((ranks, row_half), jnp.float32)
    zero_sum = (zero_back, jnp.zeros((row_half, 128), jnp.float32))

    def send_forward(layer, part, total):
        lanes = total[1]
        high = lanes.astype(jnp.bfloat16)
        low = (lanes - high.astype(jnp.float32)).astype(jnp.bfloat16)
        squares = (trail(ones, high) + trail(ones, low))[:8]
        high = squares.astype(jnp.bfloat16).astype(jnp.float32)
        partial = jnp.concatenate([total[0], high, squares - high])
        send_sum(fx_out, fx_in, fx_sem, layer, part, partial)
        return partial

    def turn(parts):
        parts = jnp.concatenate(parts)
        spare = jnp.zeros((128 - parts.shape[0], row_half), jnp.float32)
        return jnp.concatenate([parts, spare]).T

    def in_order(parts):
        wide = [part.astype(jnp.float32) for part in parts]
        straight, swapped = jnp.concatenate(wide, axis=1), jnp.concatenate(wide[::-1], axis=1)
        return jnp.where(near == 0, straight, swapped).astype(jnp.bfloat16)

    def fold(layer):
        passed(praw, psib_sem, layer)
        pbuf[layer] = (praw[layer].astype(jnp.float32) * gbuf[layer]).astype(jnp.bfloat16)

    def fold_rank(layer, raw, folded, top_by, low_by):
        def piece(t, carry):
            at = chunk(t)
            top = raw[layer, :hd, at].astype(jnp.float32)
            top = top + adapter_scale * plain(top_by, raw[layer, hd:, at])
            top = top.astype(jnp.bfloat16)
            folded[layer, :hd, at] = top
            folded[layer, hd:, at] = (adapter_scale * plain(low_by, top)).astype(jnp.bfloat16)
            return carry

        lax.fori_loop(0, chunks, piece, 0)

    def fold_into(layer):
        factor = fbuf[layer]
        fold_rank(layer, pbuf, pfold, factor[rank:, :rank], factor[:rank, hd : 2 * hd])

    def take_first(part):
        def first(t, total):
            rows = hid[0, half_rows[part], chunk(t)]
            return add(total, project(0, chunk(t), rows.astype(jnp.float32), rows))

        return send_forward(0, part, lax.fori_loop(0, chunks, first, zero_sum, unroll=True))

    def line_levels(buf, sib, wanted):
        for at_level in range(levels):

            @pl.when((lax.div(at_level, levels // 2) == lax.div(level, levels // 2)) == wanted)
            def _(at_level=at_level):
                sib_copy(buf, sib, at_level).wait_recv()

    reach = levels // 2 - 1
    for k in range(reach):
        line_arrive(x0, x_up, x_down, x_sib, k)
    for layer in range(sections):
        arrive_and_pass(p_copy, praw, psib_sem, layer)
        arrive(pa_copy, layer)
        arrive(gain_copy, layer)
        arrive(fac_copy, layer)
    fold(0)
    line_levels(x0, x_sib, True)
    partials = [take_first(0)]
    for k in range(reach, levels - 1):
        line_arrive(x0, x_up, x_down, x_sib, k)
    line_start(cot, c_up, c_down, 0)
    sib_copy(cot, c_sib, level).start()
    line_levels(x0, x_sib, False)
    partials.append(take_first(1))

    last = sections - 1
    kept, sides, backs = [], [], [None, None]
    for layer in range(sections):
        if layer == 0:
            for later in range(1, sections):
                fold(later)
                fold_into(later)
            arrive_and_pass(q_copy, qbuf, qsib_sem, 0)
            arrive(qa_copy, 0)
        if layer == 1:
            for later in range(1, sections):
                arrive_and_pass(q_copy, qbuf, qsib_sem, later)
                arrive(qa_copy, later)
        if layer < levels - 1:
            line_arrive(cot, c_up, c_down, c_sib, layer)
        passed(qbuf, qsib_sem, layer)
        if layer == last:
            for k in range(last + 1, levels - 1):
                line_arrive(cot, c_up, c_down, c_sib, k)
            for at_level in range(levels):
                sib_copy(cot, c_sib, at_level).wait_recv()
            for part in range(2):
                rows_of = half_rows[part]

                def seed(t, total_now, rows_of=rows_of):
                    at = chunk(t)
                    top = cot[rows_of, at].astype(jnp.float32) * row_weight[rows_of, :]
                    top = top.astype(jnp.bfloat16)
                    grad[last, rows_of, at] = top
                    return total_now + trail(qbuf[last, :, at], top)

                backs[part] = lax.fori_loop(0, chunks, seed, zero_back, unroll=True)
                send_sum(bx_out, bx_in, bx_sem, last, part, backs[part])
        factor = fbuf[layer]
        halves = []
        for part in range(2):
            rows_of = half_rows[part]
            whole = whole_sum(fx_out, fx_in, fx_sem, layer, part, partials[part])
            projection = whole[:ranks]
            squares = whole[ranks : ranks + 1] + whole[ranks + 8 : ranks + 9]
            inverse = lax.rsqrt(squares / width + norm_eps)
            scaled = projection * inverse
            lowrank = scaled[hd:].astype(jnp.bfloat16)
            value = (
                scaled[:hd] + adapter_scale * plain(factor[rank:, :rank], lowrank)
            ).astype(jnp.bfloat16)
            side = plain(factor[:rank, hd : 2 * hd], value).astype(jnp.bfloat16)
            mixed = jnp.concatenate(
                [value.astype(jnp.float32), adapter_scale * side.astype(jnp.float32)]
            )
            halves.append((mixed, inverse, lowrank, value, side))
            if layer < last:
                turned[part] = turn([mixed]).astype(jnp.bfloat16)

                def update(t, total_now, layer=layer, part=part, rows_of=rows_of):
                    at = chunk(t)
                    rows = hid[layer, rows_of, at].astype(jnp.float32)
                    rows = rows + plain(turned[part, :, :ranks], qbuf[layer, :, at])
                    rows = rows.astype(jnp.bfloat16)
                    hid[layer + 1, rows_of, at] = rows
                    return add(
                        total_now, project(layer + 1, at, rows.astype(jnp.float32), rows)
                    )

                total = lax.fori_loop(0, chunks, update, zero_sum, unroll=True)
                partials[part] = send_forward(layer + 1, part, total)
        kept.append(halves)
        sides.append(in_order([h[4] for h in halves]))

    def land_copy(layer, which):
        return remote(
            mine.at[layer, which],
            land.at[section, which],
            land_sem,
            layer * 2 + which,
            (layer, member),
            section * 2 + which,
        )

    def collect(layer, which, small, wide, by):
        def gather(t, carry):
            at = chunk(t)
            mine[layer, which, :, at] = (by * plain(small, wide[layer, :, at])).astype(
                jnp.bfloat16
            )
            return carry

        lax.fori_loop(0, chunks, gather, 0, unroll=True)

        @pl.when(section != layer)
        def _():
            land_copy(layer, which).start()

        @pl.when(section == layer)
        def _():
            land[layer, which] = mine[layer, which]

    collect(last, 1, sides[last], grad, adapter_scale)
    for layer in reversed(range(sections)):
        factor = fbuf[layer]
        lows, small_up, small_down = [], None, None
        wholes = []
        for part in range(2):
            rows_of = half_rows[part]
            mixed, inverse = kept[layer][part][:2]
            whole = whole_sum(bx_out, bx_in, bx_sem, layer, part, backs[part])
            wholes.append(whole)
            if layer > 0:
                correction = jnp.sum(whole * mixed, axis=0, keepdims=True) / width
                shrink = jnp.broadcast_to(inverse * inverse * correction, (8, row_half))
                columns_of = turn([whole * inverse, shrink])
                turned[part] = columns_of.astype(jnp.bfloat16)
                shrink_column = columns_of[:, ranks : ranks + 1]

                def step_back(
                    t, total_now, layer=layer, part=part, rows_of=rows_of, shrink=shrink_column
                ):
                    at = chunk(t)
                    rows = hid[layer, rows_of, at].astype(jnp.float32)
                    fresh = grad[layer, rows_of, at].astype(jnp.float32)
                    fresh = fresh + plain(turned[part, :, :ranks], pfold[layer, :, at])
                    fresh = (fresh - rows * shrink).astype(jnp.bfloat16)
                    grad[layer - 1, rows_of, at] = fresh
                    return total_now + trail(qbuf[layer - 1, :, at], fresh)

                backs[part] = lax.fori_loop(0, chunks, step_back, zero_back, unroll=True)
                send_sum(bx_out, bx_in, bx_sem, layer - 1, part, backs[part])
        for whole, (mixed, inverse, lowrank, value, side) in zip(wholes, kept[layer]):
            grad_side = (adapter_scale * whole[hd:]).astype(jnp.bfloat16)
            grad_value = (whole[:hd] + plain(factor[rank:, hd : hd + rank], grad_side)).astype(
                jnp.bfloat16
            )
            grad_low = (adapter_scale * plain(factor[:rank, :hd], grad_value)).astype(
                jnp.bfloat16
            )
            lows.append(grad_low.astype(jnp.float32) * inverse)
            up_now = trail(lowrank, grad_value)
            down_now = trail(grad_side, value)
            small_up = up_now if small_up is None else small_up + up_now
            small_down = down_now if small_down is None else small_down + down_now
        collect(layer, 0, in_order(lows), hid, 1.0)
        if layer > 0:
            collect(layer - 1, 1, sides[layer - 1], grad, adapter_scale)

        @pl.when(section == layer)
        def _(small_up=small_up, small_down=small_down):
            out_vu[...] = (adapter_scale * small_up).astype(jnp.bfloat16)
            out_od[...] = small_down.astype(jnp.bfloat16)

    def landed(source, which):
        @pl.when(section != source)
        def _():
            remote(
                mine.at[source, which],
                land.at[source, which],
                land_sem,
                source * 2 + which,
                (source, member),
                source * 2 + which,
            ).wait()

    for q in range(sections):
        landed(q, 1)
        at = pl.ds(q * columns, columns)
        out_ou[:, at] = land[q, 1]
    for j in range(sections - 1):
        for copy_of in (tok_copy, fac_copy, gain_copy, p_copy, pa_copy, q_copy, qa_copy):
            copy_of(j, section).wait_send()
        for layer in range(sections):
            for part in range(2):
                sum_copy(fx_out, fx_in, fx_sem, layer, part, j).wait_send()
                sum_copy(bx_out, bx_in, bx_sem, layer, part, j).wait_send()
    for layer in range(sections):

        @pl.when(section != layer)
        def _(layer=layer):
            sib_weight(praw, psib_sem, layer).wait_send()
            sib_weight(qbuf, qsib_sem, layer).wait_send()

    line_sent(x0, x_up, x_down, x_sib)
    line_sent(cot, c_up, c_down, c_sib)
    for q in range(sections):
        landed(q, 0)
        at = pl.ds(q * columns, columns)
        out_vd[:, at] = (land[q, 0].astype(jnp.float32) * gain[:, at]).astype(jnp.bfloat16)


def kernel_body(
    inputs,
    cotangent,
    norm_gain,
    w_value,
    w_out,
    value_down,
    value_up_factor,
    out_down,
    output_up_factor,
    block_tenant,
    valid_tokens,
    tenant_slot,
):
    sections, members = lax.axis_size("pipe"), lax.axis_size("dp")
    member = lax.axis_index("dp")
    row_count, width = inputs.shape[1:]
    micro_count = inputs.shape[0] * sections
    columns, row_total = width // sections, micro_count * row_count * members
    rank, hd = value_up_factor.shape[2:]
    ranks, row_half = hd + rank, row_total // 2
    tok = jnp.concatenate([inputs[0], cotangent[0]])
    up, down = value_up_factor[0, 0], out_down[0, 0]
    pad = ((0, 0), (0, hd - rank))
    fac = jnp.concatenate(
        [
            jnp.concatenate([up, down], axis=1),
            jnp.concatenate([jnp.pad(up.T, pad), jnp.pad(down.T, pad)], axis=1),
        ]
    )
    weight = row_weights(
        block_tenant, valid_tokens, tenant_slot, member, micro_count, row_count
    ).reshape(-1, 1)
    half_type, levels = jnp.bfloat16, members // 2
    dma = pltpu.SemaphoreType.DMA
    vmem, anywhere = pl.BlockSpec(memory_space=pltpu.VMEM), pl.BlockSpec(memory_space=pl.ANY)
    sums = sections * (sections - 1)
    outs = pl.pallas_call(
        functools.partial(columns_kernel, (sections, members)),
        out_shape=(
            jax.ShapeDtypeStruct((rank, width), half_type),
            jax.ShapeDtypeStruct((rank, hd), half_type),
            jax.ShapeDtypeStruct((rank, hd), half_type),
            jax.ShapeDtypeStruct((rank, width), half_type),
        ),
        in_specs=[anywhere] * 7 + [vmem, vmem],
        out_specs=(vmem, vmem, vmem, vmem),
        scratch_shapes=[
            pltpu.VMEM((sections, row_total, columns), half_type),
            pltpu.VMEM((sections, row_total, columns), half_type),
            pltpu.VMEM((row_total, columns), half_type),
            pltpu.VMEM((sections, 2 * row_count, columns), half_type),
            pltpu.VMEM((sections, ranks, columns), half_type),
            pltpu.VMEM((sections, ranks, columns), half_type),
            pltpu.VMEM((sections, ranks, columns), half_type),
            pltpu.VMEM((sections, ranks, columns), half_type),
            pltpu.VMEM((sections,) + fac.shape, half_type),
            pltpu.VMEM((sections, 1, columns), jnp.float32),
            pltpu.VMEM((2, row_half, 128), half_type),
            pltpu.VMEM((sections, 2, rank, columns), half_type),
            pltpu.VMEM((sections, 2, rank, columns), half_type),
            pltpu.VMEM((sections, 2, ranks + 16, row_half), half_type),
            pltpu.VMEM((sections, 2, sections - 1, ranks + 16, row_half), half_type),
            pltpu.VMEM((sections, 2, ranks, row_half), half_type),
            pltpu.VMEM((sections, 2, sections - 1, ranks, row_half), half_type),
            dma((7,)),
            dma((2, sections)),
            dma((2, sections)),
            dma((2, sections)),
            dma((2, sections)),
            dma((2, sections)),
            dma((2, sections)),
            dma((2, sections)),
            dma((2, sections)),
            dma((2, sections)),
            dma((2, levels)),
            dma((2, levels)),
            dma((2, levels)),
            dma((2, levels)),
            dma((2, levels)),
            dma((2, levels)),
            dma((2, 2 * sums)),
            dma((2, 2 * sums)),
            dma((2, 2 * sections)),
        ],
        compiler_params=pltpu.CompilerParams(
            collective_id=0, has_side_effects=True, vmem_limit_bytes=60 * 2**20
        ),
    )(
        tok,
        w_value[0],
        value_down[0, 0],
        w_out[0],
        output_up_factor[0, 0],
        norm_gain,
        fac,
        weight,
        norm_gain,
    )
    return tuple(part[None, None] for part in outs)


def solution(mesh):
    sections = mesh.shape["pipe"]

    def run(*arrays):
        depth, row_total, width = arrays[0].shape
        kept_bytes = 2 * depth * row_total * (width // sections) * sections
        chosen = kernel_body if kept_bytes <= stash_limit else relay_body
        return place(chosen)(*arrays)

    def place(chosen):
        return jax.shard_map(
            chosen,
            mesh=mesh,
            in_specs=(
                P("pipe", "dp", None),
                P("pipe", "dp", None),
                P("pipe", None),
                P("pipe", None, None),
                P("pipe", None, None),
                P("pipe", "dp", None, None),
                P("pipe", "dp", None, None),
                P("pipe", "dp", None, None),
                P("pipe", "dp", None, None),
                P(),
                P(),
                P(),
            ),
            out_specs=(
                P("pipe", "dp", None, None),
                P("pipe", "dp", None, None),
                P("pipe", "dp", None, None),
                P("pipe", "dp", None, None),
            ),
            check_vma=False,
        )

    return run
```
